128 devices in a mesh: lat: 8 (over z, x_lo), lon: 16 (over x_hi, y, core).
Axes of the slice: x: 4 (x_hi: 2, x_lo: 2; x = x_hi * 2 + x_lo), y: 4, z: 4, core: 2. Of those that a mesh axis runs over, the one named last changes fastest.
Arguments:
- latent: bfloat16 [4, 48, 384, 512], P(None, 'lat', 'lon'), may hold values from -40 to 40
- cotangent: bfloat16 [4, 48, 384, 512], P(None, 'lat', 'lon'), may hold values from -6 to 6
- qkv_weight: bfloat16 [512, 1536], replicated, may hold values from -0.25 to 0.25
- out_weight: bfloat16 [512, 512], replicated, may hold values from -0.25 to 0.25
- up_weight: bfloat16 [512, 2048], replicated, may hold values from -0.25 to 0.25
- down_weight: bfloat16 [2048, 512], replicated, may hold values from -0.125 to 0.125
- earth_bias: float32 [8, 2, 8, 20736], P('lat'), may hold values from -8 to 400
Outputs:
- out: bfloat16 [4, 48, 384, 512], P(None, 'lat', 'lon')
- grad_latent: bfloat16 [4, 48, 384, 512], P(None, 'lat', 'lon')
- weight_grad: float32 [3145728], P(('lat', 'lon'))
- bias_grad: float32 [8, 2, 8, 20736], P('lat')
The draws below stay inside these ranges and needn't reach their ends.
All inputs are finite; a program needn't handle non-finite values.
Results may differ from the reference program's by a relative error of at most 0.024.
Values may be sent and summed in bfloat16 or wider, within the bound.
No kernel may reach another device: no remote copies, remote signals or barrier semaphores. Data moves between devices by JAX's collectives and lax.ppermute only.
A program may use at most 128 MiB of HBM per device.

```python
import math
import jax
import jax.numpy as jnp
from jax import lax

D = 512
FF = 2048
HEADS = 8
LEVELS = 4
WIN_LEV = 2
WIN_LAT = 6
WIN_LON = 12
NLAT = 48
NLON = 384
WTOK = 144
LATWIN = 8


def draw_latent(key, part):
    key = jax.random.fold_in(key, 11)
    key_base, key_rows, key_cols = jax.random.split(key, 3)
    shape = (LEVELS, NLAT, NLON, D)
    row_scale = jnp.exp(jax.random.uniform(key_rows, (LEVELS, NLAT, NLON, 1), jnp.float32, math.log(0.3), math.log(3.0)))
    col_scale = jnp.exp(jax.random.uniform(key_cols, (D,), jnp.float32, math.log(0.3), math.log(3.0)))
    base = jnp.clip(jax.random.normal(key_base, shape, jnp.float32), -4.0, 4.0)
    return (base * row_scale * col_scale).astype(jnp.bfloat16)


def draw_earth_bias(key, part):
    key = jax.random.fold_in(key, 23)
    key_base = jax.random.fold_in(key, 0)
    shape = (LATWIN, LEVELS // WIN_LEV, HEADS, WTOK, WTOK)
    base = jnp.clip(jax.random.normal(key_base, shape, jnp.float32), -4.0, 4.0)
    return base.reshape(LATWIN, LEVELS // WIN_LEV, HEADS, WTOK * WTOK)


def shard_levels(stream_key, shape, shards, low, top_value):
    gain = 1.0
    for dim, parts in shards:
        steps = jax.random.uniform(jax.random.fold_in(jax.random.fold_in(stream_key, 6), dim), (parts,), jnp.float32, low / len(shards), top_value / len(shards))
        gain = gain * jnp.repeat(jnp.exp(steps), shape[dim] // parts).reshape((-1,) + (1,) * (len(shape) - 1 - dim))
    return gain


def centred(key, dims, spread, reach, shards=(), held_as=jnp.bfloat16):
    entries = jax.random.normal(key, dims, jnp.float32) * spread
    if len(shards) > 0:
        entries = shard_levels(key, dims, shards, -0.22, 0.18) * entries
    return jnp.clip(entries, min=-reach, max=reach).astype(held_as)


def setup_inputs(seed: int = 0) -> dict:
    splits = jax.random.split(jax.random.key(seed), 8)
    latent = draw_latent(jax.random.fold_in(splits[7], 71), 0)
    cotangent = centred(splits[1], (LEVELS, NLAT, NLON, D), 1.0, 6.0, ((1, 8), (2, 16)))
    qkv_weight = centred(splits[2], (D, 3 * D), D ** -0.5, 0.25)
    out_weight = centred(splits[3], (D, D), D ** -0.5, 0.25)
    up_weight = centred(splits[4], (D, FF), D ** -0.5, 0.25)
    down_weight = centred(splits[5], (FF, D), FF ** -0.5, 0.125)
    earth_bias = draw_earth_bias(jax.random.fold_in(splits[7], 71), 0)
    return dict(latent=latent, cotangent=cotangent, qkv_weight=qkv_weight, out_weight=out_weight, up_weight=up_weight, down_weight=down_weight, earth_bias=earth_bias)


norm_eps = 1e-05
masked_score = -1000000000.0

def batched(form, left, right):
    return jnp.einsum(form, left.astype(jnp.float32), right.astype(jnp.float32))

def matmul(left, right):
    return jnp.dot(left, right, preferred_element_type=jnp.float32)

def normalize(values):
    center = values - lax.optimization_barrier(jnp.mean(values, axis=-1, keepdims=True))
    inv_std = lax.rsqrt(lax.optimization_barrier(jnp.mean(center * center, axis=-1, keepdims=True)) + norm_eps)
    return (center * inv_std, inv_std)

def norm_back(normed, inv_std, upstream):
    mean_grad = lax.optimization_barrier(jnp.mean(upstream, axis=-1, keepdims=True))
    mean_prod = lax.optimization_barrier(jnp.mean(upstream * normed, axis=-1, keepdims=True))
    return inv_std * (upstream - mean_grad - normed * mean_prod)

def gelu_exact(values):
    return values * 0.5 * (1.0 + jax.scipy.special.erf(values * 0.7071067811865476))

def gelu_slope(values):
    cumulative = 0.5 * (1.0 + jax.scipy.special.erf(values * 0.7071067811865476))
    density = jnp.exp(-0.5 * values * values) * 0.3989422804014327
    return cumulative + values * density

def to_windows(field, win_lev, win_lat, win_lon):
    levels, rows, cols = field.shape[:3]
    tail = field.shape[3:]
    shaped = field.reshape((levels // win_lev, win_lev, rows // win_lat, win_lat, cols // win_lon, win_lon) + tail)
    order = (2, 0, 4, 1, 3, 5) + tuple(range(6, 6 + len(tail)))
    moved = shaped.transpose(order)
    return moved.reshape((rows // win_lat, levels // win_lev, cols // win_lon, win_lev * win_lat * win_lon) + tail)

def from_windows(windows, levels, rows, cols, win_lev, win_lat, win_lon):
    tail = windows.shape[4:]
    shaped = windows.reshape((rows // win_lat, levels // win_lev, cols // win_lon, win_lev, win_lat, win_lon) + tail)
    order = (1, 3, 0, 4, 2, 5) + tuple(range(6, 6 + len(tail)))
    return shaped.transpose(order).reshape((levels, rows, cols) + tail)

def group_codes(levels, rows, cols, row_start, total_rows, lev_shift, lat_shift):
    level_pos = lax.broadcasted_iota(jnp.int32, (levels, rows, cols), 0)
    row_pos = lax.broadcasted_iota(jnp.int32, (levels, rows, cols), 1) + row_start
    wrap_level = (level_pos >= levels - lev_shift).astype(jnp.int32)
    wrap_row = (row_pos >= total_rows - lat_shift).astype(jnp.int32)
    return 2 * wrap_level + wrap_row

def window_pass(tokens, upstream, codes, bias_rows, qkv_weight, out_weight, up_weight, down_weight, win_lev, win_lat, win_lon):
    levels, rows, cols, width = tokens.shape
    heads = bias_rows.shape[2]
    head_dim = width // heads
    win_tok = win_lev * win_lat * win_lon
    lat_wins = rows // win_lat
    lev_wins = levels // win_lev
    lon_wins = cols // win_lon
    groups = lat_wins * lev_wins * lon_wins
    count = groups * win_tok
    tok_win = to_windows(tokens, win_lev, win_lat, win_lon).reshape(count, width)
    grad_win = to_windows(upstream, win_lev, win_lat, win_lon).reshape(count, width)
    code_win = to_windows(codes, win_lev, win_lat, win_lon).reshape(groups, win_tok)
    bias_all = jnp.broadcast_to(bias_rows[:, :, None], (lat_wins, lev_wins, lon_wins, heads, win_tok * win_tok))
    bias_all = bias_all.reshape(groups, heads, win_tok, win_tok)
    scale = head_dim ** (-0.5)
    tok_float = tok_win.astype(jnp.float32)
    normed_one, inv_one = normalize(tok_float)
    normed_low = normed_one.astype(jnp.bfloat16)
    projected = matmul(normed_low, qkv_weight).astype(jnp.bfloat16)
    query = projected[:, :width].reshape(groups, win_tok, heads, head_dim)
    keys = projected[:, width:2 * width].reshape(groups, win_tok, heads, head_dim)
    values = projected[:, 2 * width:].reshape(groups, win_tok, heads, head_dim)
    scores = batched('gqhc,gkhc->ghqk', query, keys) * scale + bias_all
    allowed = code_win[:, None, :, None] == code_win[:, None, None, :]
    scores = jnp.where(allowed, scores, masked_score)
    peak = lax.optimization_barrier(jnp.max(scores, axis=-1, keepdims=True))
    expo = jnp.exp(scores - peak)
    probs = expo / lax.optimization_barrier(jnp.sum(expo, axis=-1, keepdims=True))
    probs_low = probs.astype(jnp.bfloat16)
    mixed = batched('ghqk,gkhc->gqhc', probs_low, values).reshape(count, width).astype(jnp.bfloat16)
    resid = tok_float + matmul(mixed, out_weight)
    normed_two, inv_two = normalize(resid)
    normed_low_two = normed_two.astype(jnp.bfloat16)
    hidden_pre = matmul(normed_low_two, up_weight)
    hidden_low = gelu_exact(hidden_pre).astype(jnp.bfloat16)
    result = (resid + matmul(hidden_low, down_weight)).astype(jnp.bfloat16)
    grad_float = grad_win.astype(jnp.float32)
    grad_down = matmul(hidden_low.T, grad_win)
    grad_hidden = (matmul(grad_win, down_weight.T) * gelu_slope(hidden_pre)).astype(jnp.bfloat16)
    grad_up = matmul(normed_low_two.T, grad_hidden)
    grad_resid = grad_float + norm_back(normed_two, inv_two, matmul(grad_hidden, up_weight.T))
    grad_resid_low = grad_resid.astype(jnp.bfloat16)
    grad_out = matmul(mixed.T, grad_resid_low)
    grad_mixed = matmul(grad_resid_low, out_weight.T).astype(jnp.bfloat16).reshape(groups, win_tok, heads, head_dim)
    grad_probs = batched('gqhc,gkhc->ghqk', grad_mixed, values)
    grad_values = batched('ghqk,gqhc->gkhc', probs_low, grad_mixed)
    grad_scores = probs * (grad_probs - lax.optimization_barrier(jnp.sum(grad_probs * probs, axis=-1, keepdims=True)))
    grad_scaled = (grad_scores * scale).astype(jnp.bfloat16)
    grad_query = batched('ghqk,gkhc->gqhc', grad_scaled, keys)
    grad_keys = batched('ghqk,gqhc->gkhc', grad_scaled, query)
    grad_proj = jnp.concatenate([grad_query.reshape(count, width), grad_keys.reshape(count, width), grad_values.reshape(count, width)], axis=1).astype(jnp.bfloat16)
    grad_qkv = matmul(normed_low.T, grad_proj)
    grad_tokens = (grad_resid + norm_back(normed_one, inv_one, matmul(grad_proj, qkv_weight.T))).astype(jnp.bfloat16)
    grad_bias = lax.optimization_barrier(jnp.sum(grad_scores.reshape(lat_wins, lev_wins, lon_wins, heads, win_tok * win_tok), axis=2))
    result_field = from_windows(result.reshape(lat_wins, lev_wins, lon_wins, win_tok, width), levels, rows, cols, win_lev, win_lat, win_lon)
    grad_field = from_windows(grad_tokens.reshape(lat_wins, lev_wins, lon_wins, win_tok, width), levels, rows, cols, win_lev, win_lat, win_lon)
    return (result_field, grad_field, grad_bias, (grad_qkv, grad_out, grad_up, grad_down))

def reference(latent, cotangent, qkv_weight, out_weight, up_weight, down_weight, earth_bias):
    lev_shift = WIN_LEV // 2
    lat_shift = WIN_LAT // 2
    lon_shift = WIN_LON // 2
    moved = jnp.roll(latent, (-lev_shift, -lat_shift, -lon_shift), (0, 1, 2))
    moved_grad = jnp.roll(cotangent, (-lev_shift, -lat_shift, -lon_shift), (0, 1, 2))
    zeros = (jnp.zeros((D, 3 * D), jnp.float32), jnp.zeros((D, D), jnp.float32), jnp.zeros((D, FF), jnp.float32), jnp.zeros((FF, D), jnp.float32))

    def step(carry, index):
        start = index * WIN_LAT
        tokens = lax.dynamic_slice_in_dim(moved, start, WIN_LAT, 1)
        upstream = lax.dynamic_slice_in_dim(moved_grad, start, WIN_LAT, 1)
        codes = group_codes(LEVELS, WIN_LAT, NLON, start, NLAT, lev_shift, lat_shift)
        bias_rows = lax.dynamic_slice_in_dim(earth_bias, index, 1, 0)
        result, grad_tok, grad_bias, grads = window_pass(tokens, upstream, codes, bias_rows, qkv_weight, out_weight, up_weight, down_weight, WIN_LEV, WIN_LAT, WIN_LON)
        carry = tuple((total + piece for total, piece in zip(carry, grads)))
        return (carry, (result, grad_tok, grad_bias))
    totals, stacked = lax.scan(step, zeros, jnp.arange(LATWIN, dtype=jnp.int32))
    results, grad_toks, grad_biases = stacked
    result_field = results.transpose(1, 0, 2, 3, 4).reshape(LEVELS, NLAT, NLON, D)
    grad_field = grad_toks.transpose(1, 0, 2, 3, 4).reshape(LEVELS, NLAT, NLON, D)
    out = jnp.roll(result_field, (lev_shift, lat_shift, lon_shift), (0, 1, 2))
    grad_latent = jnp.roll(grad_field, (lev_shift, lat_shift, lon_shift), (0, 1, 2))
    weight_grad = jnp.concatenate([piece.reshape(-1) for piece in totals]) * (1.0 / math.sqrt(LEVELS * NLAT * NLON))
    bias_grad = grad_biases.reshape(earth_bias.shape)
    return (out, grad_latent, weight_grad, bias_grad)
```

```python
import functools
import math

import jax
import jax.numpy as jnp
import ml_dtypes
import numpy as np
from jax import lax
from jax.experimental import pallas as pl
from jax.experimental.pallas import tpu as pltpu
from jax.sharding import PartitionSpec as P

WIDTH = 512
HIDDEN = 2048
HEADS = 8
LEVELS = 4
ROWS = 6
COLS = 24
WIN_LEV = 2
WIN_LAT = 6
WIN_LON = 12
WTOK = 144
TOKENS = LEVELS * ROWS * COLS
HALF_LAT = WIN_LAT // 2
HALF_LON = WIN_LON // 2
EDGE = 8
BAND = LEVELS * HALF_LAT * COLS
SIDE = LEVELS * HALF_LAT * EDGE
GROUP = 4
GWIDTH = GROUP * WIDTH // HEADS
GTOK = GROUP * WTOK
WINDOWS = 4
CHUNK = 48
norm_eps = 1e-05
masked_score = -1000000000.0
f32 = jnp.float32
bf16 = jnp.bfloat16


def dot(left, right):
    return lax.dot_general(left, right, (((1,), (0,)), ((), ())), preferred_element_type=f32)


def dot_nt(left, right):
    return lax.dot_general(left, right, (((1,), (1,)), ((), ())), preferred_element_type=f32)


def dot_tn(left, right):
    return lax.dot_general(left, right, (((0,), (0,)), ((), ())), preferred_element_type=f32)


def normalize(values):
    center = values - jnp.mean(values, axis=-1, keepdims=True)
    inv_std = lax.rsqrt(jnp.mean(center * center, axis=-1, keepdims=True) + norm_eps)
    return (center * inv_std, inv_std)


def norm_back(normed, inv_std, upstream):
    mean_grad = jnp.mean(upstream, axis=-1, keepdims=True)
    mean_prod = jnp.mean(upstream * normed, axis=-1, keepdims=True)
    return inv_std * (upstream - mean_grad - normed * mean_prod)


def token_tables():
    pick = np.zeros((TOKENS, TOKENS + BAND + 2 * SIDE), np.float32)
    spread = np.zeros((2 * BAND + 2 * SIDE, TOKENS), np.float32)
    for lev in range(LEVELS):
        src_lev = (lev + 1) % LEVELS
        for i in range(ROWS):
            for j in range(COLS):
                b, lv = divmod(lev, WIN_LEV)
                c, jj = divmod(j, WIN_LON)
                w = (b * 2 + c) * WTOK + (lv * WIN_LAT + i) * WIN_LON + jj
                inner_row = i < HALF_LAT
                inner_col = j < COLS - HALF_LON
                band_row = src_lev * HALF_LAT + (i if inner_row else i - HALF_LAT)
                wide = band_row * COLS + j + HALF_LON
                narrow = band_row * EDGE + j - (COLS - HALF_LON)
                if inner_row and inner_col:
                    pick[w, (src_lev * ROWS + i + HALF_LAT) * COLS + j + HALF_LON] = 1
                    spread[wide, w] = 1
                elif inner_col:
                    pick[w, TOKENS + wide] = 1
                    spread[BAND + wide, w] = 1
                elif inner_row:
                    pick[w, TOKENS + BAND + narrow] = 1
                    spread[2 * BAND + narrow, w] = 1
                else:
                    pick[w, TOKENS + BAND + SIDE + narrow] = 1
                    spread[2 * BAND + SIDE + narrow, w] = 1
    return pick.astype(ml_dtypes.bfloat16), spread.astype(ml_dtypes.bfloat16)


def loop(count, step):
    lax.fori_loop(0, count, lambda i, carry: (step(i), carry)[1], 0)


def at(index, size):
    return pl.ds(pl.multiple_of(index * size, size), size)


def gather_tokens(pick_ref, cat, own_ref, row_ref, col_ref, cor_ref):
    cat[0:TOKENS, :] = own_ref[...]
    cat[TOKENS : TOKENS + BAND, :] = row_ref[...]
    cat[TOKENS + BAND : TOKENS + BAND + SIDE, :] = col_ref[...]
    cat[TOKENS + BAND + SIDE :, :] = cor_ref[...]
    return dot(pick_ref[...], cat[...])


def head_stack(block):
    lane = lax.broadcasted_iota(jnp.int32, block.shape, 1) // (WIDTH // HEADS)
    zero = jnp.zeros_like(block)
    return jnp.concatenate([jnp.where(lane == h, block, zero) for h in range(GROUP)], axis=0)


def head_join(stacked):
    lane = lax.broadcasted_iota(jnp.int32, (WTOK, GWIDTH), 1) // (WIDTH // HEADS)
    total = stacked[0:WTOK]
    for h in range(1, GROUP):
        total = jnp.where(lane == h, stacked[h * WTOK : (h + 1) * WTOK], total)
    return total


def attend_kernel(
    pick_ref, own_ref, row_ref, col_ref, cor_ref, bias_ref, qkv_ref,
    tok_ref, proj_ref, probs_ref, mixed_ref, cat, normed, scores,
):
    scale = (WIDTH // HEADS) ** (-0.5)
    tok_ref[...] = gather_tokens(pick_ref, cat, own_ref, row_ref, col_ref, cor_ref).astype(bf16)

    def norm_rows(i):
        values, _ = normalize(tok_ref[at(i, 48), :].astype(f32))
        normed[at(i, 48), :] = values.astype(bf16)

    loop(TOKENS // 48, norm_rows)

    def project(i):
        proj_ref[:, at(i, 256)] = dot(normed[...], qkv_ref[:, at(i, 256)]).astype(bf16)

    loop(3 * WIDTH // 256, project)

    def attend(i):
        win, group = i // 2, i % 2
        rows = at(win, WTOK)
        query = head_stack(proj_ref[rows, at(group, GWIDTH)])
        scores[...] = dot_nt(query, proj_ref[rows, at(group + 2, GWIDTH)])
        for h in range(GROUP):
            part = scores[h * WTOK : (h + 1) * WTOK, :] * scale + bias_ref[(win // 2) * HEADS + group * GROUP + h]
            expo = jnp.exp(part - jnp.max(part, axis=-1, keepdims=True))
            part = expo * (1.0 / jnp.sum(expo, axis=-1, keepdims=True))
            probs_ref[i, h * WTOK : (h + 1) * WTOK, :] = part.astype(bf16)
        mixed = dot(probs_ref[i], proj_ref[rows, at(group + 4, GWIDTH)])
        mixed_ref[rows, at(group, GWIDTH)] = head_join(mixed).astype(bf16)

    loop(2 * WINDOWS, attend)


def chunk_id(dy, dx, z, place_ref, other):
    core = place_ref[0]
    core = 1 - core if other else core
    y = lax.rem(place_ref[1] + dy, 4)
    x = lax.rem(place_ref[2] + dx, 4)
    return z * 32 + lax.rem(x, 2) * 16 + (x // 2) * 8 + y * 2 + core


def put_lanes(ref, rows, value):
    for t in range(4):
        ref[t, rows, :] = value[:, t * 128 : (t + 1) * 128]


def mlp_kernel(
    place_ref, pick_ref, spread_ref, own_ref, row_ref, col_ref, cor_ref, tok_ref, mixed_ref,
    out_ref, up_ref, down_ref,
    pieces_ref, gresid_ref, keep_ref, send_ref,
    cat, grad, resid, normed, low, inv, pre, slope, hidden, ghidden, result, wgrad,
):
    grad[...] = gather_tokens(pick_ref, cat, own_ref, row_ref, col_ref, cor_ref).astype(bf16)
    resid[...] = dot(mixed_ref[...], out_ref[...])

    def norm_rows(i):
        rows = at(i, 48)
        total = tok_ref[rows, :].astype(f32) + resid[rows, :]
        resid[rows, :] = total
        values, inv_std = normalize(total)
        normed[rows, :] = values
        inv[rows, :] = jnp.broadcast_to(inv_std, (48, 128))
        low[rows, :] = values.astype(bf16)

    loop(TOKENS // 48, norm_rows)

    def feed(j):
        cols = at(j, WIDTH)
        pre[...] = dot(low[...], up_ref[:, cols])
        slope[...] = dot_nt(grad[...], down_ref[cols, :])

        def gelu(i):
            rows = at(i, 32)
            values = pre[rows, :]
            cumulative = 0.5 * (1.0 + lax.erf(values * 0.7071067811865476))
            hidden[rows, cols] = (values * cumulative).astype(bf16)
            density = jnp.exp(-0.5 * values * values) * 0.3989422804014327
            ghidden[rows, cols] = (slope[rows, :] * (cumulative + values * density)).astype(bf16)

        loop(TOKENS // 32, gelu)
        put_lanes(wgrad, at(j + 5, WIDTH), dot_tn(hidden[:, cols], grad[...]))
        put_lanes(wgrad, pl.ds(WIDTH + j, WIDTH, stride=4), dot_tn(low[...], ghidden[:, cols]))

    for j in range(HIDDEN // WIDTH):
        feed(j)

    def finish(n):
        cols = at(n, 256)
        result[:, cols] = (resid[:, cols] + dot(hidden[...], down_ref[:, cols])).astype(bf16)
        resid[:, cols] = dot_nt(ghidden[...], up_ref[cols, :])

    loop(WIDTH // 256, finish)

    def norm_rows_back(i):
        rows = at(i, 48)
        back = norm_back(normed[rows, :], inv[rows, 0:1], resid[rows, :])
        total = grad[rows, :].astype(f32) + back
        gresid_ref[rows, :] = total
        low[rows, :] = total.astype(bf16)

    loop(TOKENS // 48, norm_rows_back)
    pieces_ref[...] = dot(spread_ref[...], result[...]).astype(bf16)
    put_lanes(wgrad, slice(0, WIDTH), dot_tn(mixed_ref[...], low[...]))

    def share(i):
        dy, dx, z = i // 12, lax.rem(i // 3, 4), lax.rem(i, 3)
        for other, ref in ((False, keep_ref), (True, send_ref)):
            chunk = at(chunk_id(dy, dx, z, place_ref, other), CHUNK)
            for t in range(4):
                ref[at(i, CHUNK), t * 128 : (t + 1) * 128] = wgrad[t, chunk, :].astype(bf16)

    loop(48, share)


def attend_back_kernel(
    place_ref, proj_ref, probs_ref, gresid_ref, out_ref,
    gproj_ref, keep_ref, send_ref, gmixed, gprobs, gscores, bias,
):
    scale = (WIDTH // HEADS) ** (-0.5)
    gmixed[...] = dot_nt(gresid_ref[...].astype(bf16), out_ref[...]).astype(bf16)

    def back(i):
        lev, group = i // 2, lax.rem(i, 2)
        for c in range(2):
            win = lev * 2 + c
            rows = at(win, WTOK)
            probs = win * 2 + group
            upstream = head_stack(gmixed[rows, at(group, GWIDTH)])
            gprobs[...] = dot_nt(upstream, proj_ref[rows, at(group + 4, GWIDTH)])
            for h in range(GROUP):
                part = slice(h * WTOK, (h + 1) * WTOK)
                prob = probs_ref[probs, part, :].astype(f32)
                grads = gprobs[part, :]
                grads = prob * (grads - jnp.sum(grads * prob, axis=-1, keepdims=True))
                gscores[part, :] = (grads * scale).astype(bf16)
                if c == 0:
                    bias[lev * HEADS + group * GROUP + h] = grads
                else:
                    bias[lev * HEADS + group * GROUP + h] += grads
            gproj_ref[rows, at(group + 4, GWIDTH)] = dot_tn(probs_ref[probs], upstream).astype(bf16)
            query = head_stack(proj_ref[rows, at(group, GWIDTH)])
            gproj_ref[rows, at(group + 2, GWIDTH)] = dot_tn(gscores[...], query).astype(bf16)
            gquery = dot(gscores[...], proj_ref[rows, at(group + 2, GWIDTH)])
            gproj_ref[rows, at(group, GWIDTH)] = head_join(gquery).astype(bf16)

    loop(4, back)

    def share(i):
        head = lax.rem(place_ref[1] + i // 2, 4) * 2 + lax.rem(i, 2)
        keep_ref[i] = bias[place_ref[0] * HEADS + head].astype(bf16)
        send_ref[i] = bias[(1 - place_ref[0]) * HEADS + head].astype(bf16)

    loop(HEADS, share)


def qkv_grad_kernel(place_ref, tok_ref, gproj_ref, keep_ref, send_ref, normed, wgrad):
    def norm_rows(i):
        values, _ = normalize(tok_ref[at(i, 48), :].astype(f32))
        normed[at(i, 48), :] = values.astype(bf16)

    loop(TOKENS // 48, norm_rows)

    def product(i):
        wgrad[:, at(i, 512)] = dot_tn(normed[...], gproj_ref[:, at(i, 512)])

    loop(3, product)

    def share(i):
        dy, dx = i // 4, lax.rem(i, 4)
        for other, ref in ((False, keep_ref), (True, send_ref)):
            ref[at(i, 16), :] = wgrad[at(chunk_id(dy, dx, 0, place_ref, other), 16), :].astype(bf16)

    loop(16, share)


def token_grad_kernel(tok_ref, gproj_ref, qkv_ref, gresid_ref, spread_ref, pieces_ref, back, result):
    def product(i):
        back[:, at(i, 256)] = dot_nt(gproj_ref[...], qkv_ref[at(i, 256), :])

    loop(2, product)

    def norm_rows(i):
        rows = at(i, 48)
        values, inv_std = normalize(tok_ref[rows, :].astype(f32))
        result[rows, :] = (gresid_ref[rows, :] + norm_back(values, inv_std, back[rows, :])).astype(bf16)

    loop(TOKENS // 48, norm_rows)
    pieces_ref[...] = dot(spread_ref[...], result[...]).astype(bf16)


def call(kernel, outs, scratch, flops, *operands):
    shapes = [jax.ShapeDtypeStruct(shape, dtype) for shape, dtype in outs]
    specs = [
        pl.BlockSpec(memory_space=pltpu.SMEM if operand.dtype == jnp.int32 else pltpu.VMEM)
        for operand in operands
    ]
    return pl.pallas_call(
        kernel,
        out_shape=shapes,
        in_specs=specs,
        out_specs=[pl.BlockSpec(memory_space=pltpu.VMEM)] * len(outs),
        scratch_shapes=[pltpu.VMEM(shape, dtype) for shape, dtype in scratch],
        compiler_params=pltpu.CompilerParams(vmem_limit_bytes=50 * 2**20),
        cost_estimate=pl.CostEstimate(flops=flops, bytes_accessed=2**20, transcendentals=2**20),
    )(*operands)


def device_index(z, x, y, core):
    return z * 32 + (x % 2) * 16 + (x // 2) * 8 + y * 2 + core


def permute(value, move):
    pairs = []
    for z in range(4):
        for x in range(4):
            for y in range(4):
                for core in range(2):
                    pairs.append((device_index(z, x, y, core), device_index(*move(z, x, y, core))))
    return lax.ppermute(value, ("lat", "lon"), pairs)


def to_core(value):
    return permute(value, lambda z, x, y, core: (z, x, y, 1 - core))


def to_y(value, by):
    return permute(value, lambda z, x, y, core: (z, x, (y + by) % 4, core))


def to_x(value, by):
    return permute(value, lambda z, x, y, core: (z, (x + by) % 4, y, core))


def to_z(value, by):
    return permute(value, lambda z, x, y, core: ((z + by) % 4, x, y, core))


def to_half(value):
    return permute(value, lambda z, x, y, core: (z, (x + 2) % 4, y, core))


def shift(value, lat_by, lon_by):
    pairs = []
    for lat in range(8):
        for lon in range(16):
            pairs.append((lat * 16 + lon, (lat + lat_by) % 8 * 16 + (lon + lon_by) % 16))
    return lax.ppermute(value, ("lat", "lon"), pairs)


def total_of(parts):
    total = parts[0].astype(f32)
    for part in parts[1:]:
        total = total + part.astype(f32)
    return total


def cut(value, parts):
    size = value.shape[0] // parts
    return [value[i * size : (i + 1) * size] for i in range(parts)]


def sum_over_plane(keep, send):
    mine = [total_of(pair).astype(bf16) for pair in zip(cut(keep, 4), cut(to_core(send), 4))]
    mine = cut(total_of([mine[0]] + [to_y(mine[by], by) for by in (1, 2, 3)]).astype(bf16), 4)
    return total_of([mine[0]] + [to_x(mine[by], by) for by in (1, 2, 3)]).astype(bf16)


def halos(field):
    band = field[:, :HALF_LAT].reshape(BAND, WIDTH)
    side = field[:, HALF_LAT:, :EDGE].reshape(SIDE, WIDTH)
    corner = field[:, :HALF_LAT, :EDGE].reshape(SIDE, WIDTH)
    return [shift(band, -1, 0), shift(side, 0, -1), shift(corner, -1, -1)]


def give_back(pieces):
    stay = pieces[:BAND].reshape(LEVELS, HALF_LAT, COLS, WIDTH)
    band = shift(pieces[BAND : 2 * BAND], 1, 0).reshape(LEVELS, HALF_LAT, COLS, WIDTH)
    side = shift(pieces[2 * BAND : 2 * BAND + SIDE], 0, 1).reshape(LEVELS, HALF_LAT, EDGE, WIDTH)
    corner = shift(pieces[2 * BAND + SIDE :], 1, 1).reshape(LEVELS, HALF_LAT, EDGE, WIDTH)
    wider = ((0, 0), (0, 0), (0, COLS - EDGE), (0, 0))
    return jnp.concatenate([band + jnp.pad(corner, wider), stay + jnp.pad(side, wider)], axis=1)


def masked_bias(earth_bias):
    token = jnp.arange(WTOK, dtype=jnp.int32)
    wrap_lev = (token >= WTOK // 2).astype(jnp.int32)
    wrap_row = (token % (WTOK // 2) >= HALF_LAT * WIN_LON).astype(jnp.int32)
    wrap_row = wrap_row * (lax.axis_index("lat") == lax.axis_size("lat") - 1).astype(jnp.int32)
    codes = jnp.stack([wrap_row, 2 * wrap_lev + wrap_row])
    allowed = codes[:, :, None] == codes[:, None, :]
    bias = earth_bias.reshape(2, HEADS, WTOK, WTOK)
    return jnp.where(allowed[:, None], bias, masked_score).reshape(2 * HEADS, WTOK, WTOK)


def body(latent, cotangent, qkv_weight, out_weight, up_weight, down_weight, earth_bias):
    lat, lon = lax.axis_index("lat"), lax.axis_index("lon")
    core, y = lon % 2, (lon // 2) % 4
    x, z = (lon // 8) * 2 + lat % 2, lat // 2
    place = jnp.stack([core, y, x]).astype(jnp.int32)
    pick_table, spread_table = token_tables()
    pick, spread = jnp.asarray(pick_table), jnp.asarray(spread_table)

    near = halos(latent)
    later, near[0] = lax.optimization_barrier((cotangent, near[0]))
    grad_near = halos(later)
    tok, proj, probs, mixed = call(
        attend_kernel,
        [((TOKENS, WIDTH), bf16), ((TOKENS, 3 * WIDTH), bf16), ((8, GTOK, WTOK), bf16), ((TOKENS, WIDTH), bf16)],
        [((TOKENS + BAND + 2 * SIDE, WIDTH), bf16), ((TOKENS, WIDTH), bf16), ((GTOK, WTOK), f32)],
        4 * 10**9,
        pick, latent.reshape(TOKENS, WIDTH), *near, masked_bias(earth_bias), qkv_weight,
    )
    pieces, gresid, keep, send = call(
        mlp_kernel,
        [
            ((2 * BAND + 2 * SIDE, WIDTH), bf16), ((TOKENS, WIDTH), f32),
            ((48 * CHUNK, WIDTH), bf16), ((48 * CHUNK, WIDTH), bf16),
        ],
        [
            ((TOKENS + BAND + 2 * SIDE, WIDTH), bf16), ((TOKENS, WIDTH), bf16), ((TOKENS, WIDTH), f32),
            ((TOKENS, WIDTH), f32), ((TOKENS, WIDTH), bf16), ((TOKENS, 128), f32),
            ((TOKENS, WIDTH), f32), ((TOKENS, WIDTH), f32),
            ((TOKENS, HIDDEN), bf16), ((TOKENS, HIDDEN), bf16), ((TOKENS, WIDTH), bf16),
            ((4, 9 * WIDTH, 128), f32),
        ],
        8 * 10**9,
        place, pick, spread, cotangent.reshape(TOKENS, WIDTH), *grad_near, tok, mixed,
        out_weight, up_weight, down_weight,
    )
    gproj, bias_keep, bias_send = call(
        attend_back_kernel,
        [((TOKENS, 3 * WIDTH), bf16), ((HEADS, WTOK, WTOK), bf16), ((HEADS, WTOK, WTOK), bf16)],
        [((TOKENS, WIDTH), bf16), ((GTOK, WTOK), f32), ((GTOK, WTOK), bf16), ((2 * HEADS, WTOK, WTOK), f32)],
        6 * 10**9,
        place, proj, probs, gresid, out_weight,
    )
    qkv_keep, qkv_send = call(
        qkv_grad_kernel,
        [((256, 3 * WIDTH), bf16), ((256, 3 * WIDTH), bf16)],
        [((TOKENS, WIDTH), bf16), ((WIDTH, 3 * WIDTH), f32)],
        2 * 10**9,
        place, tok, gproj,
    )
    (grad_pieces,) = call(
        token_grad_kernel,
        [((2 * BAND + 2 * SIDE, WIDTH), bf16)],
        [((TOKENS, WIDTH), f32), ((TOKENS, WIDTH), bf16)],
        2 * 10**9,
        tok, gproj, qkv_weight, gresid, spread,
    )
    out = give_back(pieces)
    grad_latent = give_back(grad_pieces)

    others = sum_over_plane(keep, send).reshape(3, CHUNK, WIDTH)
    first = sum_over_plane(qkv_keep, qkv_send).reshape(1, CHUNK, WIDTH)
    shares = jnp.concatenate([first, others])
    ahead = [lax.dynamic_index_in_dim(shares, (z + by) % 4, 0, False) for by in range(4)]
    total = total_of([ahead[0]] + [to_z(ahead[by], by) for by in (1, 2, 3)])
    weight_grad = total.reshape(-1) * (1.0 / math.sqrt(TOKENS * lax.axis_size("lat") * lax.axis_size("lon")))

    mine = [total_of(pair).astype(bf16) for pair in zip(cut(bias_keep, 4), cut(to_core(bias_send), 4))]
    mine = total_of([mine[0]] + [to_y(mine[by], by) for by in (1, 2, 3)]).astype(bf16)
    mine = total_of([mine, to_half(mine)]).astype(bf16)
    ring = [mine] + [to_y(mine, -by) for by in (1, 2, 3)]
    ring = jnp.stack(ring + ring)
    half = lax.dynamic_slice_in_dim(ring, (4 - y) % 4, 4, 0).reshape(1, HEADS, WTOK, WTOK)
    other = to_core(half)
    both = jnp.where(core == 0, jnp.concatenate([half, other]), jnp.concatenate([other, half]))
    bias_grad = both.astype(f32).reshape(1, 2, HEADS, WTOK * WTOK)
    return (out, grad_latent, weight_grad, bias_grad)


def solution(mesh):
    field = P(None, "lat", "lon", None)
    band = P("lat", None, None, None)
    in_specs = (field, field, P(), P(), P(), P(), band)
    out_specs = (field, field, P(("lat", "lon")), band)
    return jax.shard_map(body, mesh=mesh, in_specs=in_specs, out_specs=out_specs, check_vma=False)
```

```python
import functools
import math

import jax
import jax.numpy as jnp
import ml_dtypes
import numpy as np
from jax import lax
from jax.experimental import pallas as pl
from jax.experimental.pallas import tpu as pltpu
from jax.sharding import PartitionSpec as P

WIDTH = 512
HIDDEN = 2048
HEADS = 8
LEVELS = 4
ROWS = 6
COLS = 24
WIN_LEV = 2
WIN_LAT = 6
WIN_LON = 12
WTOK = 144
TOKENS = LEVELS * ROWS * COLS
HALF_LAT = WIN_LAT // 2
HALF_LON = WIN_LON // 2
EDGE = 8
BAND = LEVELS * HALF_LAT * COLS
SIDE = LEVELS * HALF_LAT * EDGE
GROUP = 4
GWIDTH = GROUP * WIDTH // HEADS
GTOK = GROUP * WTOK
WINDOWS = 4
CHUNK = 48
norm_eps = 1e-05
masked_score = -1000000000.0
f32 = jnp.float32
bf16 = jnp.bfloat16


def dot(left, right):
    return lax.dot_general(left, right, (((1,), (0,)), ((), ())), preferred_element_type=f32)


def dot_nt(left, right):
    return lax.dot_general(left, right, (((1,), (1,)), ((), ())), preferred_element_type=f32)


def dot_tn(left, right):
    return lax.dot_general(left, right, (((0,), (0,)), ((), ())), preferred_element_type=f32)


def normalize(values):
    center = values - jnp.mean(values, axis=-1, keepdims=True)
    inv_std = lax.rsqrt(jnp.mean(center * center, axis=-1, keepdims=True) + norm_eps)
    return (center * inv_std, inv_std)


def norm_back(normed, inv_std, upstream):
    mean_grad = jnp.mean(upstream, axis=-1, keepdims=True)
    mean_prod = jnp.mean(upstream * normed, axis=-1, keepdims=True)
    return inv_std * (upstream - mean_grad - normed * mean_prod)


def token_tables():
    pick = np.zeros((TOKENS, TOKENS + BAND + 2 * SIDE), np.float32)
    spread = np.zeros((2 * BAND + 2 * SIDE, TOKENS), np.float32)
    for lev in range(LEVELS):
        src_lev = (lev + 1) % LEVELS
        for i in range(ROWS):
            for j in range(COLS):
                b, lv = divmod(lev, WIN_LEV)
                c, jj = divmod(j, WIN_LON)
                w = (b * 2 + c) * WTOK + (lv * WIN_LAT + i) * WIN_LON + jj
                inner_row = i < HALF_LAT
                inner_col = j < COLS - HALF_LON
                band_row = src_lev * HALF_LAT + (i if inner_row else i - HALF_LAT)
                wide = band_row * COLS + j + HALF_LON
                narrow = band_row * EDGE + j - (COLS - HALF_LON)
                if inner_row and inner_col:
                    pick[w, (src_lev * ROWS + i + HALF_LAT) * COLS + j + HALF_LON] = 1
                    spread[wide, w] = 1
                elif inner_col:
                    pick[w, TOKENS + wide] = 1
                    spread[BAND + wide, w] = 1
                elif inner_row:
                    pick[w, TOKENS + BAND + narrow] = 1
                    spread[2 * BAND + narrow, w] = 1
                else:
                    pick[w, TOKENS + BAND + SIDE + narrow] = 1
                    spread[2 * BAND + SIDE + narrow, w] = 1
    return pick.astype(ml_dtypes.bfloat16), spread.astype(ml_dtypes.bfloat16)


def loop(count, step):
    for i in range(count):
        step(i)


def at(index, size):
    if isinstance(index, int):
        return slice(index * size, (index + 1) * size)
    return pl.ds(pl.multiple_of(index * size, size), size)


def gather_tokens(pick_ref, cat, own_ref, row_ref, col_ref, cor_ref):
    cat[0:TOKENS, :] = own_ref[...]
    cat[TOKENS : TOKENS + BAND, :] = row_ref[...]
    cat[TOKENS + BAND : TOKENS + BAND + SIDE, :] = col_ref[...]
    cat[TOKENS + BAND + SIDE :, :] = cor_ref[...]
    return dot(pick_ref[...], cat[...])


def head_stack(block):
    lane = lax.broadcasted_iota(jnp.int32, block.shape, 1) // (WIDTH // HEADS)
    zero = jnp.zeros_like(block)
    return jnp.concatenate([jnp.where(lane == h, block, zero) for h in range(GROUP)], axis=0)


def head_join(stacked):
    lane = lax.broadcasted_iota(jnp.int32, (WTOK, GWIDTH), 1) // (WIDTH // HEADS)
    total = stacked[0:WTOK]
    for h in range(1, GROUP):
        total = jnp.where(lane == h, stacked[h * WTOK : (h + 1) * WTOK], total)
    return total


def attend_kernel(
    pick_ref, own_ref, row_ref, col_ref, cor_ref, bias_ref, qkv_ref,
    tok_ref, proj_ref, probs_ref, mixed_ref, cat, normed, scores,
):
    scale = (WIDTH // HEADS) ** (-0.5)
    tok_ref[...] = gather_tokens(pick_ref, cat, own_ref, row_ref, col_ref, cor_ref).astype(bf16)

    def norm_rows(i):
        values, _ = normalize(tok_ref[at(i, 48), :].astype(f32))
        normed[at(i, 48), :] = values.astype(bf16)

    loop(TOKENS // 48, norm_rows)

    def project(i):
        proj_ref[:, at(i, 256)] = dot(normed[...], qkv_ref[:, at(i, 256)]).astype(bf16)

    loop(3 * WIDTH // 256, project)

    def attend(i):
        win, group = i // 2, i % 2
        rows = at(win, WTOK)
        query = head_stack(proj_ref[rows, at(group, GWIDTH)])
        scores[...] = dot_nt(query, proj_ref[rows, at(group + 2, GWIDTH)])
        for h in range(GROUP):
            part = scores[h * WTOK : (h + 1) * WTOK, :] * scale + bias_ref[(win // 2) * HEADS + group * GROUP + h]
            expo = jnp.exp(part - jnp.max(part, axis=-1, keepdims=True))
            part = expo * (1.0 / jnp.sum(expo, axis=-1, keepdims=True))
            probs_ref[i, h * WTOK : (h + 1) * WTOK, :] = part.astype(bf16)
        mixed = dot(probs_ref[i], proj_ref[rows, at(group + 4, GWIDTH)])
        mixed_ref[rows, at(group, GWIDTH)] = head_join(mixed).astype(bf16)

    loop(2 * WINDOWS, attend)


def chunk_id(dy, dx, z, place_ref, other):
    core = place_ref[0]
    core = 1 - core if other else core
    y = lax.rem(place_ref[1] + dy, 4)
    x = lax.rem(place_ref[2] + dx, 4)
    return z * 32 + lax.rem(x, 2) * 16 + (x // 2) * 8 + y * 2 + core


def put_lanes(ref, rows, value):
    for t in range(4):
        ref[t, rows, :] = value[:, t * 128 : (t + 1) * 128]


def mlp_kernel(
    place_ref, pick_ref, spread_ref, own_ref, row_ref, col_ref, cor_ref, tok_ref, mixed_ref,
    out_ref, up_ref, down_ref,
    pieces_ref, gresid_ref, keep_ref, send_ref,
    cat, grad, resid, normed, low, inv, pre, slope, hidden, ghidden, result, wgrad,
):
    grad[...] = gather_tokens(pick_ref, cat, own_ref, row_ref, col_ref, cor_ref).astype(bf16)
    resid[...] = dot(mixed_ref[...], out_ref[...])

    def norm_rows(i):
        rows = at(i, 48)
        total = tok_ref[rows, :].astype(f32) + resid[rows, :]
        resid[rows, :] = total
        values, inv_std = normalize(total)
        normed[rows, :] = values
        inv[rows, :] = jnp.broadcast_to(inv_std, (48, 128))
        low[rows, :] = values.astype(bf16)

    loop(TOKENS // 48, norm_rows)

    def feed(j):
        cols = at(j, WIDTH)
        pre[...] = dot(low[...], up_ref[:, cols])
        slope[...] = dot_nt(grad[...], down_ref[cols, :])

        def gelu(i):
            rows = at(i, 32)
            values = pre[rows, :]
            cumulative = 0.5 * (1.0 + lax.erf(values * 0.7071067811865476))
            hidden[rows, cols] = (values * cumulative).astype(bf16)
            density = jnp.exp(-0.5 * values * values) * 0.3989422804014327
            ghidden[rows, cols] = (slope[rows, :] * (cumulative + values * density)).astype(bf16)

        loop(TOKENS // 32, gelu)
        put_lanes(wgrad, at(j + 5, WIDTH), dot_tn(hidden[:, cols], grad[...]))
        put_lanes(wgrad, pl.ds(WIDTH + j, WIDTH, stride=4), dot_tn(low[...], ghidden[:, cols]))

    for j in range(HIDDEN // WIDTH):
        feed(j)

    def finish(n):
        cols = at(n, 256)
        result[:, cols] = (resid[:, cols] + dot(hidden[...], down_ref[:, cols])).astype(bf16)
        resid[:, cols] = dot_nt(ghidden[...], up_ref[cols, :])

    loop(WIDTH // 256, finish)

    def norm_rows_back(i):
        rows = at(i, 48)
        back = norm_back(normed[rows, :], inv[rows, 0:1], resid[rows, :])
        total = grad[rows, :].astype(f32) + back
        gresid_ref[rows, :] = total
        low[rows, :] = total.astype(bf16)

    loop(TOKENS // 48, norm_rows_back)
    pieces_ref[...] = dot(spread_ref[...], result[...]).astype(bf16)
    put_lanes(wgrad, slice(0, WIDTH), dot_tn(mixed_ref[...], low[...]))

    def share(i):
        outer, inner, z = i // 12, i // 3 % 4, i % 3
        for other, ref in ((False, keep_ref), (True, send_ref)):
            for t in range(4):
                order = (outer, inner) if t < 2 else (inner, outer)
                chunk = at(chunk_id(*order, z, place_ref, other), CHUNK)
                ref[at(i, CHUNK), t * 128 : (t + 1) * 128] = wgrad[t, chunk, :].astype(bf16)

    loop(48, share)


def attend_back_kernel(
    place_ref, proj_ref, probs_ref, gresid_ref, out_ref,
    gproj_ref, keep_ref, send_ref, gmixed, gprobs, gscores, bias,
):
    scale = (WIDTH // HEADS) ** (-0.5)
    gmixed[...] = dot_nt(gresid_ref[...].astype(bf16), out_ref[...]).astype(bf16)

    def back(i):
        lev, group = i // 2, i % 2
        for c in range(2):
            win = lev * 2 + c
            rows = at(win, WTOK)
            probs = win * 2 + group
            upstream = head_stack(gmixed[rows, at(group, GWIDTH)])
            gprobs[...] = dot_nt(upstream, proj_ref[rows, at(group + 4, GWIDTH)])
            for h in range(GROUP):
                part = slice(h * WTOK, (h + 1) * WTOK)
                prob = probs_ref[probs, part, :].astype(f32)
                grads = gprobs[part, :]
                grads = prob * (grads - jnp.sum(grads * prob, axis=-1, keepdims=True))
                gscores[part, :] = (grads * scale).astype(bf16)
                if c == 0:
                    bias[lev * HEADS + group * GROUP + h] = grads
                else:
                    bias[lev * HEADS + group * GROUP + h] += grads
            gproj_ref[rows, at(group + 4, GWIDTH)] = dot_tn(probs_ref[probs], upstream).astype(bf16)
            query = head_stack(proj_ref[rows, at(group, GWIDTH)])
            gproj_ref[rows, at(group + 2, GWIDTH)] = dot_tn(gscores[...], query).astype(bf16)
            gquery = dot(gscores[...], proj_ref[rows, at(group + 2, GWIDTH)])
            gproj_ref[rows, at(group, GWIDTH)] = head_join(gquery).astype(bf16)

    loop(4, back)

    def share(i):
        head = lax.rem(place_ref[1] + i // 2, 4) * 2 + i % 2
        keep_ref[i] = bias[place_ref[0] * HEADS + head].astype(bf16)
        send_ref[i] = bias[(1 - place_ref[0]) * HEADS + head].astype(bf16)

    loop(HEADS, share)


def qkv_grad_kernel(place_ref, tok_ref, gproj_ref, keep_ref, send_ref, normed, wgrad):
    def norm_rows(i):
        values, _ = normalize(tok_ref[at(i, 48), :].astype(f32))
        normed[at(i, 48), :] = values.astype(bf16)

    loop(TOKENS // 48, norm_rows)

    def product(i):
        wgrad[:, at(i, 512)] = dot_tn(normed[...], gproj_ref[:, at(i, 512)])

    loop(3, product)

    def share(i):
        for other, ref in ((False, keep_ref), (True, send_ref)):
            for half, order in enumerate(((i // 4, i % 4), (i % 4, i // 4))):
                chunk = at(chunk_id(*order, 0, place_ref, other), 16)
                for block in range(3):
                    rows = pl.ds(pl.multiple_of(i * CHUNK + block * 16, 16), 16)
                    left = block * WIDTH + half * 256
                    ref[rows, half * 256 : half * 256 + 256] = wgrad[chunk, left : left + 256].astype(bf16)

    loop(16, share)


def token_grad_kernel(tok_ref, gproj_ref, qkv_ref, gresid_ref, spread_ref, pieces_ref, back, result):
    def product(i):
        back[:, at(i, 256)] = dot_nt(gproj_ref[...], qkv_ref[at(i, 256), :])

    loop(2, product)

    def norm_rows(i):
        rows = at(i, 48)
        values, inv_std = normalize(tok_ref[rows, :].astype(f32))
        result[rows, :] = (gresid_ref[rows, :] + norm_back(values, inv_std, back[rows, :])).astype(bf16)

    loop(TOKENS // 48, norm_rows)
    pieces_ref[...] = dot(spread_ref[...], result[...]).astype(bf16)


def call(kernel, outs, scratch, *operands, vmem=16):
    shapes = [jax.ShapeDtypeStruct(shape, dtype) for shape, dtype in outs]
    specs = [
        pl.BlockSpec(memory_space=pltpu.SMEM if operand.dtype == jnp.int32 else pltpu.VMEM)
        for operand in operands
    ]
    return pl.pallas_call(
        kernel,
        out_shape=shapes,
        in_specs=specs,
        out_specs=[pl.BlockSpec(memory_space=pltpu.VMEM)] * len(outs),
        scratch_shapes=[pltpu.VMEM(shape, dtype) for shape, dtype in scratch],
        compiler_params=pltpu.CompilerParams(vmem_limit_bytes=vmem * 2**20),
        cost_estimate=pl.CostEstimate(flops=2**20, bytes_accessed=2**16, transcendentals=0),
    )(*operands)


def device_index(z, x, y, core):
    return z * 32 + (x % 2) * 16 + (x // 2) * 8 + y * 2 + core


def permute(value, move):
    pairs = []
    for z in range(4):
        for x in range(4):
            for y in range(4):
                for core in range(2):
                    pairs.append((device_index(z, x, y, core), device_index(*move(z, x, y, core))))
    return lax.ppermute(value, ("lat", "lon"), pairs)


def to_core(value):
    return permute(value, lambda z, x, y, core: (z, x, y, 1 - core))


def to_y(value, by):
    return permute(value, lambda z, x, y, core: (z, x, (y + by) % 4, core))


def to_x(value, by):
    return permute(value, lambda z, x, y, core: (z, (x + by) % 4, y, core))


def to_z(value, by):
    return permute(value, lambda z, x, y, core: ((z + by) % 4, x, y, core))


def to_half(value):
    return permute(value, lambda z, x, y, core: (z, (x + 2) % 4, y, core))


def shift(value, lat_by, lon_by):
    pairs = []
    for lat in range(8):
        for lon in range(16):
            pairs.append((lat * 16 + lon, (lat + lat_by) % 8 * 16 + (lon + lon_by) % 16))
    return lax.ppermute(value, ("lat", "lon"), pairs)


def total_of(parts):
    total = parts[0].astype(f32)
    for part in parts[1:]:
        total = total + part.astype(f32)
    return total


def cut(value, parts):
    size = value.shape[0] // parts
    return [value[i * size : (i + 1) * size] for i in range(parts)]


def spread_out(parts, move):
    return [parts[0]] + [move(parts[by], by) for by in (1, 2, 3)]


def core_sum(keep, arrived, cols=slice(None)):
    return [total_of(pair).astype(bf16) for pair in zip(cut(keep[:, cols], 4), cut(arrived[:, cols], 4))]


def low_sum(parts):
    return total_of(parts).astype(bf16)


def after(values, others):
    leaves, tree = jax.tree.flatten((values, others))
    return jax.tree.unflatten(tree, lax.optimization_barrier(leaves))


def halos(field):
    band = field[:, :HALF_LAT].reshape(BAND, WIDTH)
    side = field[:, HALF_LAT:, :EDGE].reshape(SIDE, WIDTH)
    corner = field[:, :HALF_LAT, :EDGE].reshape(SIDE, WIDTH)
    return [shift(band, -1, 0), shift(side, 0, -1), shift(corner, -1, -1)]


def give_back(pieces):
    return [
        pieces[:BAND],
        shift(pieces[BAND : 2 * BAND], 1, 0),
        shift(pieces[2 * BAND : 2 * BAND + SIDE], 0, 1),
        shift(pieces[2 * BAND + SIDE :], 1, 1),
    ]


def assemble(parts):
    stay, band = (part.reshape(LEVELS, HALF_LAT, COLS, WIDTH) for part in parts[:2])
    side, corner = (part.reshape(LEVELS, HALF_LAT, EDGE, WIDTH) for part in parts[2:])
    wider = ((0, 0), (0, 0), (0, COLS - EDGE), (0, 0))
    return jnp.concatenate([band + jnp.pad(corner, wider), stay + jnp.pad(side, wider)], axis=1)


def masked_bias(earth_bias):
    token = jnp.arange(WTOK, dtype=jnp.int32)
    wrap_lev = (token >= WTOK // 2).astype(jnp.int32)
    wrap_row = (token % (WTOK // 2) >= HALF_LAT * WIN_LON).astype(jnp.int32)
    wrap_row = wrap_row * (lax.axis_index("lat") == lax.axis_size("lat") - 1).astype(jnp.int32)
    codes = jnp.stack([wrap_row, 2 * wrap_lev + wrap_row])
    allowed = codes[:, :, None] == codes[:, None, :]
    bias = earth_bias.reshape(2, HEADS, WTOK, WTOK)
    return jnp.where(allowed[:, None], bias, masked_score).reshape(2 * HEADS, WTOK, WTOK)


def body(latent, cotangent, qkv_weight, out_weight, up_weight, down_weight, earth_bias):
    lat, lon = lax.axis_index("lat"), lax.axis_index("lon")
    core, y = lon % 2, (lon // 2) % 4
    x, z = (lon // 8) * 2 + lat % 2, lat // 2
    place = jnp.stack([core, y, x]).astype(jnp.int32)
    pick_table, spread_table = token_tables()
    pick, spread = jnp.asarray(pick_table), jnp.asarray(spread_table)

    near = halos(latent)
    later, near[0] = lax.optimization_barrier((cotangent, near[0]))
    grad_near = halos(later)
    tok, proj, probs, mixed = call(
        attend_kernel,
        [((TOKENS, WIDTH), bf16), ((TOKENS, 3 * WIDTH), bf16), ((8, GTOK, WTOK), bf16), ((TOKENS, WIDTH), bf16)],
        [((TOKENS + BAND + 2 * SIDE, WIDTH), bf16), ((TOKENS, WIDTH), bf16), ((GTOK, WTOK), f32)],
        pick, latent.reshape(TOKENS, WIDTH), *near, masked_bias(earth_bias), qkv_weight,
    )
    pieces, gresid, keep, send = call(
        mlp_kernel,
        [
            ((2 * BAND + 2 * SIDE, WIDTH), bf16), ((TOKENS, WIDTH), f32),
            ((48 * CHUNK, WIDTH), bf16), ((48 * CHUNK, WIDTH), bf16),
        ],
        [
            ((TOKENS + BAND + 2 * SIDE, WIDTH), bf16), ((TOKENS, WIDTH), bf16), ((TOKENS, WIDTH), f32),
            ((TOKENS, WIDTH), f32), ((TOKENS, WIDTH), bf16), ((TOKENS, 128), f32),
            ((TOKENS, WIDTH), f32), ((TOKENS, WIDTH), f32),
            ((TOKENS, HIDDEN), bf16), ((TOKENS, HIDDEN), bf16), ((TOKENS, WIDTH), bf16),
            ((4, 9 * WIDTH, 128), f32),
        ],
        place, pick, spread, cotangent.reshape(TOKENS, WIDTH), *grad_near, tok, mixed,
        out_weight, up_weight, down_weight, vmem=40,
    )
    arrived, returned = to_core(send), give_back(pieces)
    gproj, bias_keep, bias_send = call(
        attend_back_kernel,
        [((TOKENS, 3 * WIDTH), bf16), ((HEADS, WTOK, WTOK), bf16), ((HEADS, WTOK, WTOK), bf16)],
        [((TOKENS, WIDTH), bf16), ((GTOK, WTOK), f32), ((GTOK, WTOK), bf16), ((2 * HEADS, WTOK, WTOK), f32)],
        place, proj, probs, gresid, out_weight,
    )
    (gproj, bias_send), (arrived, returned) = after((gproj, bias_send), (arrived, returned))
    bias_arrived = to_core(bias_send)
    qkv_keep, qkv_send = call(
        qkv_grad_kernel,
        [((16 * CHUNK, WIDTH), bf16), ((16 * CHUNK, WIDTH), bf16)],
        [((TOKENS, WIDTH), bf16), ((WIDTH, 3 * WIDTH), f32)],
        place, tok, gproj,
    )
    (gproj, qkv_send), bias_arrived = after((gproj, qkv_send), bias_arrived)
    qkv_arrived = to_core(qkv_send)
    bias_parts = spread_out(core_sum(bias_keep, bias_arrived), to_y)
    (grad_pieces,) = call(
        token_grad_kernel,
        [((2 * BAND + 2 * SIDE, WIDTH), bf16)],
        [((TOKENS, WIDTH), f32), ((TOKENS, WIDTH), bf16)],
        tok, gproj, qkv_weight, gresid, spread,
    )
    grad_pieces, qkv_arrived = after((grad_pieces, qkv_arrived), ())[0]
    left, right = (
        spread_out(
            [
                jnp.concatenate(pair)
                for pair in zip(core_sum(qkv_keep, qkv_arrived, cols), core_sum(keep, arrived, cols))
            ],
            move,
        )
        for cols, move in ((slice(0, 256), to_y), (slice(256, 512), to_x))
    )
    grad_returned = give_back(grad_pieces)
    mine = low_sum(bias_parts)
    bias_half = [mine, to_half(mine)]
    bias_half, left, right = after((bias_half, left, right), ())[0]
    left, right = (
        spread_out([jnp.concatenate(pair) for pair in zip(cut(total[:192], 4), cut(total[192:], 4))], move)
        for total, move in ((low_sum(left), to_x), (low_sum(right), to_y))
    )
    mine = low_sum(bias_half)
    ring = [mine] + [to_y(mine, -by) for by in (1, 2, 3)]
    ring, left, right, grad_returned = after((ring, left, right, grad_returned), ())[0]
    shares = jnp.concatenate([low_sum(left), low_sum(right)], axis=1).reshape(4, CHUNK, WIDTH)
    total = total_of(spread_out([lax.dynamic_index_in_dim(shares, (z + by) % 4, 0, False) for by in range(4)], to_z))
    by_row = total.reshape(3, 16, WIDTH).transpose(1, 0, 2).reshape(CHUNK, WIDTH)
    total = jnp.where(z == 0, by_row, total)
    weight_grad = total.reshape(-1) * (1.0 / math.sqrt(TOKENS * lax.axis_size("lat") * lax.axis_size("lon")))

    ring = jnp.stack(ring + ring)
    half = lax.dynamic_slice_in_dim(ring, (4 - y) % 4, 4, 0).reshape(1, HEADS, WTOK, WTOK)
    other = to_core(half)
    both = jnp.where(core == 0, jnp.concatenate([half, other]), jnp.concatenate([other, half]))
    bias_grad = both.astype(f32).reshape(1, 2, HEADS, WTOK * WTOK)
    out, grad_latent = assemble(returned), assemble(grad_returned)
    return (out, grad_latent, weight_grad, bias_grad)


def solution(mesh):
    field = P(None, "lat", "lon", None)
    band = P("lat", None, None, None)
    in_specs = (field, field, P(), P(), P(), P(), band)
    out_specs = (field, field, P(("lat", "lon")), band)
    return jax.shard_map(body, mesh=mesh, in_specs=in_specs, out_specs=out_specs, check_vma=False)
```

```python
import functools
import math

import jax
import jax.numpy as jnp
import ml_dtypes
import numpy as np
from jax import lax
from jax.experimental import pallas as pl
from jax.experimental.pallas import tpu as pltpu
from jax.sharding import PartitionSpec as P

WIDTH = 512
HIDDEN = 2048
HEADS = 8
LEVELS = 4
ROWS = 6
COLS = 24
WIN_LEV = 2
WIN_LAT = 6
WIN_LON = 12
WTOK = 144
TOKENS = LEVELS * ROWS * COLS
HALF_LAT = WIN_LAT // 2
HALF_LON = WIN_LON // 2
EDGE = 8
BAND = LEVELS * HALF_LAT * COLS
SIDE = LEVELS * HALF_LAT * EDGE
GROUP = 4
GWIDTH = GROUP * WIDTH // HEADS
GTOK = GROUP * WTOK
WINDOWS = 4
CHUNK = 48
norm_eps = 1e-05
masked_score = -1000000000.0
f32 = jnp.float32
bf16 = jnp.bfloat16


def dot(left, right):
    return lax.dot_general(left, right, (((1,), (0,)), ((), ())), preferred_element_type=f32)


def dot_nt(left, right):
    return lax.dot_general(left, right, (((1,), (1,)), ((), ())), preferred_element_type=f32)


def dot_tn(left, right):
    return lax.dot_general(left, right, (((0,), (0,)), ((), ())), preferred_element_type=f32)


def normalize(values):
    center = values - jnp.mean(values, axis=-1, keepdims=True)
    inv_std = lax.rsqrt(jnp.mean(center * center, axis=-1, keepdims=True) + norm_eps)
    return (center * inv_std, inv_std)


def norm_back(normed, inv_std, upstream):
    mean_grad = jnp.mean(upstream, axis=-1, keepdims=True)
    mean_prod = jnp.mean(upstream * normed, axis=-1, keepdims=True)
    return inv_std * (upstream - mean_grad - normed * mean_prod)


def token_tables():
    pick = np.zeros((TOKENS, TOKENS + BAND + 2 * SIDE), np.float32)
    spread = np.zeros((2 * BAND + 2 * SIDE, TOKENS), np.float32)
    for lev in range(LEVELS):
        src_lev = (lev + 1) % LEVELS
        for i in range(ROWS):
            for j in range(COLS):
                b, lv = divmod(lev, WIN_LEV)
                c, jj = divmod(j, WIN_LON)
                w = (b * 2 + c) * WTOK + (lv * WIN_LAT + i) * WIN_LON + jj
                inner_row = i < HALF_LAT
                inner_col = j < COLS - HALF_LON
                band_row = src_lev * HALF_LAT + (i if inner_row else i - HALF_LAT)
                wide = band_row * COLS + j + HALF_LON
                narrow = band_row * EDGE + j - (COLS - HALF_LON)
                if inner_row and inner_col:
                    pick[w, (src_lev * ROWS + i + HALF_LAT) * COLS + j + HALF_LON] = 1
                    spread[wide, w] = 1
                elif inner_col:
                    pick[w, TOKENS + wide] = 1
                    spread[BAND + wide, w] = 1
                elif inner_row:
                    pick[w, TOKENS + BAND + narrow] = 1
                    spread[2 * BAND + narrow, w] = 1
                else:
                    pick[w, TOKENS + BAND + SIDE + narrow] = 1
                    spread[2 * BAND + SIDE + narrow, w] = 1
    return pick.astype(ml_dtypes.bfloat16), spread.astype(ml_dtypes.bfloat16)


def loop(count, step):
    for i in range(count):
        step(i)


def at(index, size):
    if isinstance(index, int):
        return slice(index * size, (index + 1) * size)
    return pl.ds(pl.multiple_of(index * size, size), size)


def gather_tokens(pick_ref, cat, own_ref, row_ref, col_ref, cor_ref):
    cat[0:TOKENS, :] = own_ref[...]
    cat[TOKENS : TOKENS + BAND, :] = row_ref[...]
    cat[TOKENS + BAND : TOKENS + BAND + SIDE, :] = col_ref[...]
    cat[TOKENS + BAND + SIDE :, :] = cor_ref[...]
    return dot(pick_ref[...], cat[...])


def head_stack(block):
    lane = lax.broadcasted_iota(jnp.int32, block.shape, 1) // (WIDTH // HEADS)
    zero = jnp.zeros_like(block)
    return jnp.concatenate([jnp.where(lane == h, block, zero) for h in range(GROUP)], axis=0)


def head_join(stacked):
    lane = lax.broadcasted_iota(jnp.int32, (WTOK, GWIDTH), 1) // (WIDTH // HEADS)
    total = stacked[0:WTOK]
    for h in range(1, GROUP):
        total = jnp.where(lane == h, stacked[h * WTOK : (h + 1) * WTOK], total)
    return total


def attend_kernel(
    pick_ref, own_ref, row_ref, col_ref, cor_ref, bias_ref, qkv_ref,
    tok_ref, proj_ref, probs_ref, mixed_ref, cat, normed, scores,
):
    scale = (WIDTH // HEADS) ** (-0.5)
    tok_ref[...] = gather_tokens(pick_ref, cat, own_ref, row_ref, col_ref, cor_ref).astype(bf16)

    def norm_rows(i):
        values, _ = normalize(tok_ref[at(i, 48), :].astype(f32))
        normed[at(i, 48), :] = values.astype(bf16)

    loop(TOKENS // 48, norm_rows)

    def project(i):
        proj_ref[:, at(i, 256)] = dot(normed[...], qkv_ref[:, at(i, 256)]).astype(bf16)

    loop(3 * WIDTH // 256, project)

    def attend(i):
        win, group = i // 2, i % 2
        rows = at(win, WTOK)
        query = head_stack(proj_ref[rows, at(group, GWIDTH)])
        scores[...] = dot_nt(query, proj_ref[rows, at(group + 2, GWIDTH)])
        for h in range(GROUP):
            part = scores[h * WTOK : (h + 1) * WTOK, :] * scale + bias_ref[(win // 2) * HEADS + group * GROUP + h]
            expo = jnp.exp(part - jnp.max(part, axis=-1, keepdims=True))
            part = expo * (1.0 / jnp.sum(expo, axis=-1, keepdims=True))
            probs_ref[i, h * WTOK : (h + 1) * WTOK, :] = part.astype(bf16)
        mixed = dot(probs_ref[i], proj_ref[rows, at(group + 4, GWIDTH)])
        mixed_ref[rows, at(group, GWIDTH)] = head_join(mixed).astype(bf16)

    loop(2 * WINDOWS, attend)


def chunk_id(outer, inner, z, place_ref, other):
    core = 1 - place_ref[0] if other else place_ref[0]
    y = lax.rem(place_ref[1] + outer + core * (inner - outer), 4)
    x = lax.rem(place_ref[2] + inner + core * (outer - inner), 4)
    return z * 32 + lax.rem(x, 2) * 16 + (x // 2) * 8 + y * 2 + core


def put_lanes(ref, rows, value):
    for t in range(4):
        ref[t, rows, :] = value[:, t * 128 : (t + 1) * 128]


def mlp_kernel(
    place_ref, pick_ref, spread_ref, own_ref, row_ref, col_ref, cor_ref, tok_ref, mixed_ref,
    out_ref, up_ref, down_ref,
    pieces_ref, gresid_ref, keep_ref, send_ref,
    cat, grad, resid, normed, low, inv, pre, slope, hidden, ghidden, result, wgrad,
):
    grad[...] = gather_tokens(pick_ref, cat, own_ref, row_ref, col_ref, cor_ref).astype(bf16)
    resid[...] = dot(mixed_ref[...], out_ref[...])

    def norm_rows(i):
        rows = at(i, 48)
        total = tok_ref[rows, :].astype(f32) + resid[rows, :]
        resid[rows, :] = total
        values, inv_std = normalize(total)
        normed[rows, :] = values
        inv[rows, :] = jnp.broadcast_to(inv_std, (48, 128))
        low[rows, :] = values.astype(bf16)

    loop(TOKENS // 48, norm_rows)

    def feed(j):
        cols = at(j, WIDTH)
        pre[...] = dot(low[...], up_ref[:, cols])
        slope[...] = dot_nt(grad[...], down_ref[cols, :])

        def gelu(i):
            rows = at(i, 32)
            values = pre[rows, :]
            cumulative = 0.5 * (1.0 + lax.erf(values * 0.7071067811865476))
            hidden[rows, cols] = (values * cumulative).astype(bf16)
            density = jnp.exp(-0.5 * values * values) * 0.3989422804014327
            ghidden[rows, cols] = (slope[rows, :] * (cumulative + values * density)).astype(bf16)

        loop(TOKENS // 32, gelu)
        put_lanes(wgrad, at(j + 5, WIDTH), dot_tn(hidden[:, cols], grad[...]))
        put_lanes(wgrad, pl.ds(WIDTH + j, WIDTH, stride=4), dot_tn(low[...], ghidden[:, cols]))

    for j in range(HIDDEN // WIDTH):
        feed(j)

    def finish(n):
        cols = at(n, 256)
        result[:, cols] = (resid[:, cols] + dot(hidden[...], down_ref[:, cols])).astype(bf16)
        resid[:, cols] = dot_nt(ghidden[...], up_ref[cols, :])

    loop(WIDTH // 256, finish)

    def norm_rows_back(i):
        rows = at(i, 48)
        back = norm_back(normed[rows, :], inv[rows, 0:1], resid[rows, :])
        total = grad[rows, :].astype(f32) + back
        gresid_ref[rows, :] = total
        low[rows, :] = total.astype(bf16)

    loop(TOKENS // 48, norm_rows_back)
    pieces_ref[...] = dot(spread_ref[...], result[...]).astype(bf16)
    put_lanes(wgrad, slice(0, WIDTH), dot_tn(mixed_ref[...], low[...]))

    def share(i):
        for other, ref in ((False, keep_ref), (True, send_ref)):
            chunk = at(chunk_id(i // 12, i // 3 % 4, i % 3, place_ref, other), CHUNK)
            for t in range(4):
                ref[at(i, CHUNK), t * 128 : (t + 1) * 128] = wgrad[t, chunk, :].astype(bf16)

    loop(48, share)


def attend_back_kernel(
    place_ref, proj_ref, probs_ref, gresid_ref, out_ref,
    gproj_ref, keep_ref, send_ref, gmixed, gprobs, gscores, bias, tail,
):
    scale = (WIDTH // HEADS) ** (-0.5)
    gmixed[...] = dot_nt(gresid_ref[...].astype(bf16), out_ref[...]).astype(bf16)

    def back(i):
        lev, group = i // 2, i % 2
        for c in range(2):
            win = lev * 2 + c
            rows = at(win, WTOK)
            probs = win * 2 + group
            upstream = head_stack(gmixed[rows, at(group, GWIDTH)])
            gprobs[...] = dot_nt(upstream, proj_ref[rows, at(group + 4, GWIDTH)])
            for h in range(GROUP):
                part = slice(h * WTOK, (h + 1) * WTOK)
                prob = probs_ref[probs, part, :].astype(f32)
                grads = gprobs[part, :]
                grads = prob * (grads - jnp.sum(grads * prob, axis=-1, keepdims=True))
                gscores[part, :] = (grads * scale).astype(bf16)
                if c == 0:
                    bias[lev * HEADS + group * GROUP + h] = grads
                else:
                    bias[lev * HEADS + group * GROUP + h] += grads
            gproj_ref[rows, at(group + 4, GWIDTH)] = dot_tn(probs_ref[probs], upstream).astype(bf16)
            query = head_stack(proj_ref[rows, at(group, GWIDTH)])
            gproj_ref[rows, at(group + 2, GWIDTH)] = dot_tn(gscores[...], query).astype(bf16)
            gquery = dot(gscores[...], proj_ref[rows, at(group + 2, GWIDTH)])
            gproj_ref[rows, at(group, GWIDTH)] = head_join(gquery).astype(bf16)

    loop(4, back)

    for ref, lev in ((keep_ref, place_ref[0]), (send_ref, 1 - place_ref[0])):
        for h in range(HEADS):
            part = bias[lev * HEADS + h]
            ref[h * WTOK : (h + 1) * WTOK, :] = part[:, :128].astype(bf16)
            tail[:, h * 16 : (h + 1) * 16] = part[:, 128:]
        ref[HEADS * WTOK :, :] = tail[...].astype(bf16)


def qkv_grad_kernel(place_ref, tok_ref, gproj_ref, keep_ref, send_ref, normed, wgrad):
    def norm_rows(i):
        values, _ = normalize(tok_ref[at(i, 48), :].astype(f32))
        normed[at(i, 48), :] = values.astype(bf16)

    loop(TOKENS // 48, norm_rows)

    def product(i):
        wgrad[:, at(i, 512)] = dot_tn(normed[...], gproj_ref[:, at(i, 512)])

    loop(3, product)

    def share(i):
        for other, ref in ((False, keep_ref), (True, send_ref)):
            chunk = at(chunk_id(i // 4, i % 4, 0, place_ref, other), 16)
            for block in range(3):
                ref[at(i * 3 + block, 16), :] = wgrad[chunk, block * WIDTH : (block + 1) * WIDTH].astype(bf16)

    loop(16, share)


def token_grad_kernel(tok_ref, gproj_ref, qkv_ref, gresid_ref, spread_ref, pieces_ref, back, result):
    def product(i):
        back[:, at(i, 256)] = dot_nt(gproj_ref[...], qkv_ref[at(i, 256), :])

    loop(2, product)

    def norm_rows(i):
        rows = at(i, 48)
        values, inv_std = normalize(tok_ref[rows, :].astype(f32))
        result[rows, :] = (gresid_ref[rows, :] + norm_back(values, inv_std, back[rows, :])).astype(bf16)

    loop(TOKENS // 48, norm_rows)
    pieces_ref[...] = dot(spread_ref[...], result[...]).astype(bf16)


def call(kernel, outs, scratch, *operands, vmem=12):
    shapes = [jax.ShapeDtypeStruct(shape, dtype) for shape, dtype in outs]
    specs = [
        pl.BlockSpec(memory_space=pltpu.SMEM if operand.dtype == jnp.int32 else pltpu.VMEM)
        for operand in operands
    ]
    return pl.pallas_call(
        kernel,
        out_shape=shapes,
        in_specs=specs,
        out_specs=[pl.BlockSpec(memory_space=pltpu.VMEM)] * len(outs),
        scratch_shapes=[pltpu.VMEM(shape, dtype) for shape, dtype in scratch],
        compiler_params=pltpu.CompilerParams(vmem_limit_bytes=vmem * 2**20),
        cost_estimate=pl.CostEstimate(flops=2**20, bytes_accessed=2**16, transcendentals=0),
    )(*operands)


def device_index(z, x, y, core):
    return z * 32 + (x % 2) * 16 + (x // 2) * 8 + y * 2 + core


def permute(value, move):
    pairs = []
    for z in range(4):
        for x in range(4):
            for y in range(4):
                for core in range(2):
                    pairs.append((device_index(z, x, y, core), device_index(*move(z, x, y, core))))
    return lax.ppermute(value, ("lat", "lon"), pairs)


def to_core(value):
    return permute(value, lambda z, x, y, core: (z, x, y, 1 - core))


def stage(value, first, by):
    def move(z, x, y, core):
        return (z, x, (y + by) % 4, core) if (core == 0) == first else (z, (x + by) % 4, y, core)

    return permute(value, move)


def to_z(value, by):
    return permute(value, lambda z, x, y, core: ((z + by) % 4, x, y, core))


def bias_step(value, step):
    def move(z, x, y, core):
        kind = (step + 2 * core) % 3
        return ((z, x, y ^ 1, core), (z, x, 3 - y, core), (z, (x + 2) % 4, y, core))[kind]

    return low_sum([value, permute(value, move)])


def shift(value, lat_by, lon_by):
    pairs = []
    for lat in range(8):
        for lon in range(16):
            pairs.append((lat * 16 + lon, (lat + lat_by) % 8 * 16 + (lon + lon_by) % 16))
    return lax.ppermute(value, ("lat", "lon"), pairs)


def total_of(parts):
    total = parts[0].astype(f32)
    for part in parts[1:]:
        total = total + part.astype(f32)
    return total


def cut(value, parts):
    size = value.shape[0] // parts
    return [value[i * size : (i + 1) * size] for i in range(parts)]


def spread_out(parts, move):
    return [parts[0]] + [move(parts[by], by) for by in (1, 2, 3)]


def spread_stage(parts, first):
    return spread_out(parts, lambda value, by: stage(value, first, by))


def core_sum(keep, arrived):
    return [low_sum(pair) for pair in zip(cut(keep, 4), cut(arrived, 4))]


def low_sum(parts):
    return total_of(parts).astype(bf16)


def after(values, others):
    leaves, tree = jax.tree.flatten((values, others))
    return jax.tree.unflatten(tree, lax.optimization_barrier(leaves))


def halos(field):
    band = field[:, :HALF_LAT].reshape(BAND, WIDTH)
    side = field[:, HALF_LAT:, :EDGE].reshape(SIDE, WIDTH)
    corner = field[:, :HALF_LAT, :EDGE].reshape(SIDE, WIDTH)
    return [shift(band, -1, 0), shift(side, 0, -1), shift(corner, -1, -1)]


def give_back(pieces):
    return [
        pieces[:BAND],
        shift(pieces[BAND : 2 * BAND], 1, 0),
        shift(pieces[2 * BAND : 2 * BAND + SIDE], 0, 1),
        shift(pieces[2 * BAND + SIDE :], 1, 1),
    ]


def assemble(parts):
    stay, band = (part.reshape(LEVELS, HALF_LAT, COLS, WIDTH) for part in parts[:2])
    side, corner = (part.reshape(LEVELS, HALF_LAT, EDGE, WIDTH) for part in parts[2:])
    wider = ((0, 0), (0, 0), (0, COLS - EDGE), (0, 0))
    return jnp.concatenate([band + jnp.pad(corner, wider), stay + jnp.pad(side, wider)], axis=1)


def masked_bias(earth_bias):
    token = jnp.arange(WTOK, dtype=jnp.int32)
    wrap_lev = (token >= WTOK // 2).astype(jnp.int32)
    wrap_row = (token % (WTOK // 2) >= HALF_LAT * WIN_LON).astype(jnp.int32)
    wrap_row = wrap_row * (lax.axis_index("lat") == lax.axis_size("lat") - 1).astype(jnp.int32)
    codes = jnp.stack([wrap_row, 2 * wrap_lev + wrap_row])
    allowed = codes[:, :, None] == codes[:, None, :]
    bias = earth_bias.reshape(2, HEADS, WTOK, WTOK)
    return jnp.where(allowed[:, None], bias, masked_score).reshape(2 * HEADS, WTOK, WTOK)


def body(latent, cotangent, qkv_weight, out_weight, up_weight, down_weight, earth_bias):
    lat, lon = lax.axis_index("lat"), lax.axis_index("lon")
    core, y = lon % 2, (lon // 2) % 4
    x, z = (lon // 8) * 2 + lat % 2, lat // 2
    place = jnp.stack([core, y, x]).astype(jnp.int32)
    pick_table, spread_table = token_tables()
    pick, spread = jnp.asarray(pick_table), jnp.asarray(spread_table)

    bias = masked_bias(earth_bias)
    near, grad_near = halos(latent), halos(cotangent)
    tok, proj, probs, mixed = call(
        attend_kernel,
        [((TOKENS, WIDTH), bf16), ((TOKENS, 3 * WIDTH), bf16), ((8, GTOK, WTOK), bf16), ((TOKENS, WIDTH), bf16)],
        [((TOKENS + BAND + 2 * SIDE, WIDTH), bf16), ((TOKENS, WIDTH), bf16), ((GTOK, WTOK), f32)],
        pick, latent.reshape(TOKENS, WIDTH), *near, bias, qkv_weight,
    )
    pieces, gresid, keep, send = call(
        mlp_kernel,
        [
            ((2 * BAND + 2 * SIDE, WIDTH), bf16), ((TOKENS, WIDTH), f32),
            ((48 * CHUNK, WIDTH), bf16), ((48 * CHUNK, WIDTH), bf16),
        ],
        [
            ((TOKENS + BAND + 2 * SIDE, WIDTH), bf16), ((TOKENS, WIDTH), bf16), ((TOKENS, WIDTH), f32),
            ((TOKENS, WIDTH), f32), ((TOKENS, WIDTH), bf16), ((TOKENS, 128), f32),
            ((TOKENS, WIDTH), f32), ((TOKENS, WIDTH), f32),
            ((TOKENS, HIDDEN), bf16), ((TOKENS, HIDDEN), bf16), ((TOKENS, WIDTH), bf16),
            ((4, 9 * WIDTH, 128), f32),
        ],
        place, pick, spread, cotangent.reshape(TOKENS, WIDTH), *grad_near, tok, mixed,
        out_weight, up_weight, down_weight, vmem=24,
    )
    arrived, returned = to_core(send), give_back(pieces)
    gproj, bias_keep, bias_send = call(
        attend_back_kernel,
        [((TOKENS, 3 * WIDTH), bf16), ((9 * WTOK, 128), bf16), ((9 * WTOK, 128), bf16)],
        [((TOKENS, WIDTH), bf16), ((GTOK, WTOK), f32), ((GTOK, WTOK), bf16), ((2 * HEADS, WTOK, WTOK), f32), ((WTOK, 128), f32)],
        place, proj, probs, gresid, out_weight,
    )
    (gproj, bias_send), (arrived, returned) = after((gproj, bias_send), (arrived, returned))
    bias_arrived = to_core(bias_send)
    others = spread_stage(core_sum(keep, arrived), True)
    qkv_keep, qkv_send = call(
        qkv_grad_kernel,
        [((16 * CHUNK, WIDTH), bf16), ((16 * CHUNK, WIDTH), bf16)],
        [((TOKENS, WIDTH), bf16), ((WIDTH, 3 * WIDTH), f32)],
        place, tok, gproj,
    )
    qkv_arrived = to_core(qkv_send)
    bias_mine = bias_step(low_sum([bias_keep, bias_arrived]), 0)
    gproj, qkv_arrived, bias_mine, others = after((gproj, qkv_arrived, bias_mine, others), ())[0]
    first = spread_stage(core_sum(qkv_keep, qkv_arrived), True)
    bias_mine = bias_step(bias_mine, 1)
    (grad_pieces,) = call(
        token_grad_kernel,
        [((2 * BAND + 2 * SIDE, WIDTH), bf16)],
        [((TOKENS, WIDTH), f32), ((TOKENS, WIDTH), bf16)],
        tok, gproj, qkv_weight, gresid, spread,
    )
    first, grad_pieces, bias_mine = after((first, grad_pieces, bias_mine), ())[0]
    parts = [jnp.concatenate(pair) for pair in zip(cut(low_sum(first), 4), cut(low_sum(others), 4))]
    parts = spread_stage(parts, False)
    bias_mine = bias_step(bias_mine, 2)
    grad_returned = give_back(grad_pieces)
    parts, bias_mine = after((parts, bias_mine), ())[0]
    shares = low_sum(parts).reshape(4, CHUNK, WIDTH)
    bias_other = to_core(bias_mine)
    total = total_of(spread_out([lax.dynamic_index_in_dim(shares, (z + by) % 4, 0, False) for by in range(4)], to_z))
    by_row = total.reshape(3, 16, WIDTH).transpose(1, 0, 2).reshape(CHUNK, WIDTH)
    total = jnp.where(z == 0, by_row, total)
    weight_grad = total.reshape(-1) * (1.0 / math.sqrt(TOKENS * lax.axis_size("lat") * lax.axis_size("lon")))

    both = jnp.stack([jnp.where(core == 0, bias_mine, bias_other), jnp.where(core == 0, bias_other, bias_mine)])
    wide = both[:, : HEADS * WTOK].reshape(2, HEADS, WTOK, 128)
    tail = both[:, HEADS * WTOK :].reshape(2, WTOK, HEADS, 16).transpose(0, 2, 1, 3)
    bias_grad = jnp.concatenate([wide, tail], axis=3).astype(f32).reshape(1, 2, HEADS, WTOK * WTOK)
    out, grad_latent = assemble(returned), assemble(grad_returned)
    return (out, grad_latent, weight_grad, bias_grad)


def solution(mesh):
    field = P(None, "lat", "lon", None)
    band = P("lat", None, None, None)
    in_specs = (field, field, P(), P(), P(), P(), band)
    out_specs = (field, field, P(("lat", "lon")), band)
    return jax.shard_map(body, mesh=mesh, in_specs=in_specs, out_specs=out_specs, check_vma=False)
```

```python
import functools
import math

import jax
import jax.numpy as jnp
import ml_dtypes
import numpy as np
from jax import lax
from jax.experimental import pallas as pl
from jax.experimental.pallas import tpu as pltpu
from jax.sharding import PartitionSpec as P

WIDTH = 512
HIDDEN = 2048
HEADS = 8
LEVELS = 4
ROWS = 6
COLS = 24
WIN_LEV = 2
WIN_LAT = 6
WIN_LON = 12
WTOK = 144
TOKENS = LEVELS * ROWS * COLS
HALF_LAT = WIN_LAT // 2
HALF_LON = WIN_LON // 2
EDGE = 8
BAND = LEVELS * HALF_LAT * COLS
SIDE = LEVELS * HALF_LAT * EDGE
GROUP = 4
GWIDTH = GROUP * WIDTH // HEADS
GTOK = GROUP * WTOK
WINDOWS = 4
CHUNK = 48
norm_eps = 1e-05
masked_score = -1000000000.0
f32 = jnp.float32
bf16 = jnp.bfloat16


def dot(left, right):
    return lax.dot_general(left, right, (((1,), (0,)), ((), ())), preferred_element_type=f32)


def dot_nt(left, right):
    return lax.dot_general(left, right, (((1,), (1,)), ((), ())), preferred_element_type=f32)


def dot_tn(left, right):
    return lax.dot_general(left, right, (((0,), (0,)), ((), ())), preferred_element_type=f32)


def normalize(values):
    center = values - jnp.mean(values, axis=-1, keepdims=True)
    inv_std = lax.rsqrt(jnp.mean(center * center, axis=-1, keepdims=True) + norm_eps)
    return (center * inv_std, inv_std)


def norm_back(normed, inv_std, upstream):
    mean_grad = jnp.mean(upstream, axis=-1, keepdims=True)
    mean_prod = jnp.mean(upstream * normed, axis=-1, keepdims=True)
    return inv_std * (upstream - mean_grad - normed * mean_prod)


def token_tables():
    pick = np.zeros((TOKENS, TOKENS + BAND + 2 * SIDE), np.float32)
    spread = np.zeros((2 * BAND + 2 * SIDE, TOKENS), np.float32)
    for lev in range(LEVELS):
        src_lev = (lev + 1) % LEVELS
        for i in range(ROWS):
            for j in range(COLS):
                b, lv = divmod(lev, WIN_LEV)
                c, jj = divmod(j, WIN_LON)
                w = (b * 2 + c) * WTOK + (lv * WIN_LAT + i) * WIN_LON + jj
                inner_row = i < HALF_LAT
                inner_col = j < COLS - HALF_LON
                band_row = src_lev * HALF_LAT + (i if inner_row else i - HALF_LAT)
                wide = band_row * COLS + j + HALF_LON
                narrow = band_row * EDGE + j - (COLS - HALF_LON)
                if inner_row and inner_col:
                    pick[w, (src_lev * ROWS + i + HALF_LAT) * COLS + j + HALF_LON] = 1
                    spread[wide, w] = 1
                elif inner_col:
                    pick[w, TOKENS + wide] = 1
                    spread[BAND + wide, w] = 1
                elif inner_row:
                    pick[w, TOKENS + BAND + narrow] = 1
                    spread[2 * BAND + narrow, w] = 1
                else:
                    pick[w, TOKENS + BAND + SIDE + narrow] = 1
                    spread[2 * BAND + SIDE + narrow, w] = 1
    return pick.astype(ml_dtypes.bfloat16), spread.astype(ml_dtypes.bfloat16)


def loop(count, step):
    for i in range(count):
        step(i)


def at(index, size):
    if isinstance(index, int):
        return slice(index * size, (index + 1) * size)
    return pl.ds(pl.multiple_of(index * size, size), size)


def gather_tokens(pick_ref, cat, own_ref, row_ref, col_ref, cor_ref):
    cat[0:TOKENS, :] = own_ref[...]
    cat[TOKENS : TOKENS + BAND, :] = row_ref[...]
    cat[TOKENS + BAND : TOKENS + BAND + SIDE, :] = col_ref[...]
    cat[TOKENS + BAND + SIDE :, :] = cor_ref[...]
    return dot(pick_ref[...], cat[...])


def head_stack(block):
    lane = lax.broadcasted_iota(jnp.int32, block.shape, 1) // (WIDTH // HEADS)
    zero = jnp.zeros_like(block)
    return jnp.concatenate([jnp.where(lane == h, block, zero) for h in range(GROUP)], axis=0)


def head_join(stacked):
    lane = lax.broadcasted_iota(jnp.int32, (WTOK, GWIDTH), 1) // (WIDTH // HEADS)
    total = stacked[0:WTOK]
    for h in range(1, GROUP):
        total = jnp.where(lane == h, stacked[h * WTOK : (h + 1) * WTOK], total)
    return total


def attend_kernel(
    pick_ref, own_ref, row_ref, col_ref, cor_ref, bias_ref, qkv_ref,
    tok_ref, proj_ref, probs_ref, mixed_ref, cat, normed, scores,
):
    scale = (WIDTH // HEADS) ** (-0.5)
    tok_ref[...] = gather_tokens(pick_ref, cat, own_ref, row_ref, col_ref, cor_ref).astype(bf16)

    def norm_rows(i):
        values, _ = normalize(tok_ref[at(i, 48), :].astype(f32))
        normed[at(i, 48), :] = values.astype(bf16)

    loop(TOKENS // 48, norm_rows)

    def project(i):
        proj_ref[:, at(i, 256)] = dot(normed[...], qkv_ref[:, at(i, 256)]).astype(bf16)

    loop(3 * WIDTH // 256, project)

    def attend(i):
        win, group = i // 2, i % 2
        rows = at(win, WTOK)
        query = head_stack(proj_ref[rows, at(group, GWIDTH)])
        scores[...] = dot_nt(query, proj_ref[rows, at(group + 2, GWIDTH)])
        for h in range(GROUP):
            part = scores[h * WTOK : (h + 1) * WTOK, :] * scale + bias_ref[(win // 2) * HEADS + group * GROUP + h]
            expo = jnp.exp(part - jnp.max(part, axis=-1, keepdims=True))
            part = expo * (1.0 / jnp.sum(expo, axis=-1, keepdims=True))
            probs_ref[i, h * WTOK : (h + 1) * WTOK, :] = part.astype(bf16)
        mixed = dot(probs_ref[i], proj_ref[rows, at(group + 4, GWIDTH)])
        mixed_ref[rows, at(group, GWIDTH)] = head_join(mixed).astype(bf16)

    loop(2 * WINDOWS, attend)


def chunk_id(outer, inner, z, place_ref, other):
    core = 1 - place_ref[0] if other else place_ref[0]
    y = lax.rem(place_ref[1] + outer + core * (inner - outer), 4)
    x = lax.rem(place_ref[2] + inner + core * (outer - inner), 4)
    return z * 32 + lax.rem(x, 2) * 16 + (x // 2) * 8 + y * 2 + core


def put_lanes(ref, rows, value):
    for t in range(4):
        ref[t, rows, :] = value[:, t * 128 : (t + 1) * 128]


def mlp_kernel(
    place_ref, pick_ref, spread_ref, own_ref, row_ref, col_ref, cor_ref, tok_ref, mixed_ref,
    out_ref, up_ref, down_ref,
    pieces_ref, gresid_ref, keep_ref, send_ref,
    cat, grad, resid, normed, low, inv, pre, slope, hidden, ghidden, result, wgrad,
):
    grad[...] = gather_tokens(pick_ref, cat, own_ref, row_ref, col_ref, cor_ref).astype(bf16)
    resid[...] = dot(mixed_ref[...], out_ref[...])

    def norm_rows(i):
        rows = at(i, 48)
        total = tok_ref[rows, :].astype(f32) + resid[rows, :]
        resid[rows, :] = total
        values, inv_std = normalize(total)
        normed[rows, :] = values
        inv[rows, :] = jnp.broadcast_to(inv_std, (48, 128))
        low[rows, :] = values.astype(bf16)

    loop(TOKENS // 48, norm_rows)

    def feed(j):
        cols = at(j, WIDTH)
        pre[...] = dot(low[...], up_ref[:, cols])
        slope[...] = dot_nt(grad[...], down_ref[cols, :])

        def gelu(i):
            rows = at(i, 32)
            values = pre[rows, :]
            cumulative = 0.5 * (1.0 + lax.erf(values * 0.7071067811865476))
            hidden[rows, cols] = (values * cumulative).astype(bf16)
            density = jnp.exp(-0.5 * values * values) * 0.3989422804014327
            ghidden[rows, cols] = (slope[rows, :] * (cumulative + values * density)).astype(bf16)

        loop(TOKENS // 32, gelu)
        put_lanes(wgrad, at(j + 5, WIDTH), dot_tn(hidden[:, cols], grad[...]))
        put_lanes(wgrad, pl.ds(WIDTH + j, WIDTH, stride=4), dot_tn(low[...], ghidden[:, cols]))

    for j in range(HIDDEN // WIDTH):
        feed(j)

    def finish(n):
        cols = at(n, 256)
        result[:, cols] = (resid[:, cols] + dot(hidden[...], down_ref[:, cols])).astype(bf16)
        resid[:, cols] = dot_nt(ghidden[...], up_ref[cols, :])

    loop(WIDTH // 256, finish)

    def norm_rows_back(i):
        rows = at(i, 48)
        back = norm_back(normed[rows, :], inv[rows, 0:1], resid[rows, :])
        total = grad[rows, :].astype(f32) + back
        gresid_ref[rows, :] = total
        low[rows, :] = total.astype(bf16)

    loop(TOKENS // 48, norm_rows_back)
    pieces_ref[...] = dot(spread_ref[...], result[...]).astype(bf16)
    put_lanes(wgrad, slice(0, WIDTH), dot_tn(mixed_ref[...], low[...]))

    def share(i):
        for other, ref in ((False, keep_ref), (True, send_ref)):
            chunk = at(chunk_id(i // 12, i // 3 % 4, i % 3, place_ref, other), CHUNK)
            for t in range(4):
                ref[at(i, CHUNK), t * 128 : (t + 1) * 128] = wgrad[t, chunk, :].astype(bf16)

    loop(48, share)


def attend_back_kernel(
    place_ref, proj_ref, probs_ref, gresid_ref, out_ref,
    gproj_ref, keep_ref, send_ref, gmixed, gprobs, gscores, bias, tail,
):
    scale = (WIDTH // HEADS) ** (-0.5)
    gmixed[...] = dot_nt(gresid_ref[...].astype(bf16), out_ref[...]).astype(bf16)

    def back(i):
        lev, group = i // 2, i % 2
        for c in range(2):
            win = lev * 2 + c
            rows = at(win, WTOK)
            probs = win * 2 + group
            upstream = head_stack(gmixed[rows, at(group, GWIDTH)])
            gprobs[...] = dot_nt(upstream, proj_ref[rows, at(group + 4, GWIDTH)])
            for h in range(GROUP):
                part = slice(h * WTOK, (h + 1) * WTOK)
                prob = probs_ref[probs, part, :].astype(f32)
                grads = gprobs[part, :]
                grads = prob * (grads - jnp.sum(grads * prob, axis=-1, keepdims=True))
                gscores[part, :] = (grads * scale).astype(bf16)
                if c == 0:
                    bias[lev * HEADS + group * GROUP + h] = grads
                else:
                    bias[lev * HEADS + group * GROUP + h] += grads
            gproj_ref[rows, at(group + 4, GWIDTH)] = dot_tn(probs_ref[probs], upstream).astype(bf16)
            query = head_stack(proj_ref[rows, at(group, GWIDTH)])
            gproj_ref[rows, at(group + 2, GWIDTH)] = dot_tn(gscores[...], query).astype(bf16)
            gquery = dot(gscores[...], proj_ref[rows, at(group + 2, GWIDTH)])
            gproj_ref[rows, at(group, GWIDTH)] = head_join(gquery).astype(bf16)

    loop(4, back)

    for ref, lev in ((keep_ref, place_ref[0]), (send_ref, 1 - place_ref[0])):
        for h in range(HEADS):
            part = bias[lev * HEADS + h]
            ref[h * WTOK : (h + 1) * WTOK, :] = part[:, :128].astype(bf16)
            tail[:, h * 16 : (h + 1) * 16] = part[:, 128:]
        ref[HEADS * WTOK :, :] = tail[...].astype(bf16)


def qkv_grad_kernel(place_ref, tok_ref, gproj_ref, keep_ref, send_ref, normed, wgrad):
    def norm_rows(i):
        values, _ = normalize(tok_ref[at(i, 48), :].astype(f32))
        normed[at(i, 48), :] = values.astype(bf16)

    loop(TOKENS // 48, norm_rows)

    def product(i):
        wgrad[:, at(i, 512)] = dot_tn(normed[...], gproj_ref[:, at(i, 512)])

    loop(3, product)

    def share(i):
        for other, ref in ((False, keep_ref), (True, send_ref)):
            chunk = at(chunk_id(i // 4, i % 4, 0, place_ref, other), 16)
            for block in range(3):
                ref[at(i * 3 + block, 16), :] = wgrad[chunk, block * WIDTH : (block + 1) * WIDTH].astype(bf16)

    loop(16, share)


def token_grad_kernel(tok_ref, gproj_ref, qkv_ref, gresid_ref, spread_ref, pieces_ref, back, result):
    def product(i):
        back[:, at(i, 256)] = dot_nt(gproj_ref[...], qkv_ref[at(i, 256), :])

    loop(2, product)

    def norm_rows(i):
        rows = at(i, 48)
        values, inv_std = normalize(tok_ref[rows, :].astype(f32))
        result[rows, :] = (gresid_ref[rows, :] + norm_back(values, inv_std, back[rows, :])).astype(bf16)

    loop(TOKENS // 48, norm_rows)
    pieces_ref[...] = dot(spread_ref[...], result[...]).astype(bf16)


def call(kernel, outs, scratch, *operands, vmem=12):
    shapes = [jax.ShapeDtypeStruct(shape, dtype) for shape, dtype in outs]
    specs = [
        pl.BlockSpec(memory_space=pltpu.SMEM if operand.dtype == jnp.int32 else pltpu.VMEM)
        for operand in operands
    ]
    return pl.pallas_call(
        kernel,
        out_shape=shapes,
        in_specs=specs,
        out_specs=[pl.BlockSpec(memory_space=pltpu.VMEM)] * len(outs),
        scratch_shapes=[pltpu.VMEM(shape, dtype) for shape, dtype in scratch],
        compiler_params=pltpu.CompilerParams(vmem_limit_bytes=vmem * 2**20),
        cost_estimate=pl.CostEstimate(flops=2**20, bytes_accessed=2**16, transcendentals=0),
    )(*operands)


def device_index(z, x, y, core):
    return z * 32 + (x % 2) * 16 + (x // 2) * 8 + y * 2 + core


def permute(value, move):
    pairs = []
    for z in range(4):
        for x in range(4):
            for y in range(4):
                for core in range(2):
                    pairs.append((device_index(z, x, y, core), device_index(*move(z, x, y, core))))
    return lax.ppermute(value, ("lat", "lon"), pairs)


def to_core(value):
    return permute(value, lambda z, x, y, core: (z, x, y, 1 - core))


def stage(value, first, by):
    def move(z, x, y, core):
        return (z, x, (y + by) % 4, core) if (core == 0) == first else (z, (x + by) % 4, y, core)

    return permute(value, move)


def to_z(value, by):
    return permute(value, lambda z, x, y, core: ((z + by) % 4, x, y, core))


def bias_step(value, step):
    def move(z, x, y, core):
        kind = (step + 2 * core) % 3
        return ((z, x, y ^ 1, core), (z, x, 3 - y, core), (z, (x + 2) % 4, y, core))[kind]

    return low_sum([value, permute(value, move)])


def shift(value, lat_by, lon_by):
    pairs = []
    for lat in range(8):
        for lon in range(16):
            pairs.append((lat * 16 + lon, (lat + lat_by) % 8 * 16 + (lon + lon_by) % 16))
    return lax.ppermute(value, ("lat", "lon"), pairs)


def total_of(parts):
    total = parts[0].astype(f32)
    for part in parts[1:]:
        total = total + part.astype(f32)
    return total


def cut(value, parts):
    size = value.shape[0] // parts
    return [value[i * size : (i + 1) * size] for i in range(parts)]


def spread_out(parts, move):
    return [parts[0]] + [move(parts[by], by) for by in (1, 2, 3)]


def spread_stage(parts, first):
    return spread_out(parts, lambda value, by: stage(value, first, by))


def core_sum(keep, arrived):
    return [low_sum(pair) for pair in zip(cut(keep, 4), cut(arrived, 4))]


def low_sum(parts):
    return total_of(parts).astype(bf16)


def after(values, others):
    leaves, tree = jax.tree.flatten((values, others))
    return jax.tree.unflatten(tree, lax.optimization_barrier(leaves))


def halos(field):
    band = field[:, :HALF_LAT].reshape(BAND, WIDTH)
    side = field[:, HALF_LAT:, :EDGE].reshape(SIDE, WIDTH)
    corner = field[:, :HALF_LAT, :EDGE].reshape(SIDE, WIDTH)
    return [shift(band, -1, 0), shift(side, 0, -1), shift(corner, -1, -1)]


def give_back(pieces):
    return [
        pieces[:BAND],
        shift(pieces[BAND : 2 * BAND], 1, 0),
        shift(pieces[2 * BAND : 2 * BAND + SIDE], 0, 1),
        shift(pieces[2 * BAND + SIDE :], 1, 1),
    ]


def assemble(parts):
    stay, band = (part.reshape(LEVELS, HALF_LAT, COLS, WIDTH) for part in parts[:2])
    side, corner = (part.reshape(LEVELS, HALF_LAT, EDGE, WIDTH) for part in parts[2:])
    wider = ((0, 0), (0, 0), (0, COLS - EDGE), (0, 0))
    return jnp.concatenate([band + jnp.pad(corner, wider), stay + jnp.pad(side, wider)], axis=1)


def masked_bias(earth_bias):
    token = jnp.arange(WTOK, dtype=jnp.int32)
    wrap_lev = (token >= WTOK // 2).astype(jnp.int32)
    wrap_row = (token % (WTOK // 2) >= HALF_LAT * WIN_LON).astype(jnp.int32)
    wrap_row = wrap_row * (lax.axis_index("lat") == lax.axis_size("lat") - 1).astype(jnp.int32)
    codes = jnp.stack([wrap_row, 2 * wrap_lev + wrap_row])
    allowed = codes[:, :, None] == codes[:, None, :]
    bias = earth_bias.reshape(2, HEADS, WTOK, WTOK)
    return jnp.where(allowed[:, None], bias, masked_score).reshape(2 * HEADS, WTOK, WTOK)


def body(latent, cotangent, qkv_weight, out_weight, up_weight, down_weight, earth_bias):
    lat, lon = lax.axis_index("lat"), lax.axis_index("lon")
    core, y = lon % 2, (lon // 2) % 4
    x, z = (lon // 8) * 2 + lat % 2, lat // 2
    place = jnp.stack([core, y, x]).astype(jnp.int32)
    pick_table, spread_table = token_tables()
    pick, spread = jnp.asarray(pick_table), jnp.asarray(spread_table)

    bias = masked_bias(earth_bias)
    near, grad_near = halos(latent), halos(cotangent)
    tok, proj, probs, mixed = call(
        attend_kernel,
        [((TOKENS, WIDTH), bf16), ((TOKENS, 3 * WIDTH), bf16), ((8, GTOK, WTOK), bf16), ((TOKENS, WIDTH), bf16)],
        [((TOKENS + BAND + 2 * SIDE, WIDTH), bf16), ((TOKENS, WIDTH), bf16), ((GTOK, WTOK), f32)],
        pick, latent.reshape(TOKENS, WIDTH), *near, bias, qkv_weight,
    )
    pieces, gresid, keep, send = call(
        mlp_kernel,
        [
            ((2 * BAND + 2 * SIDE, WIDTH), bf16), ((TOKENS, WIDTH), f32),
            ((48 * CHUNK, WIDTH), bf16), ((48 * CHUNK, WIDTH), bf16),
        ],
        [
            ((TOKENS + BAND + 2 * SIDE, WIDTH), bf16), ((TOKENS, WIDTH), bf16), ((TOKENS, WIDTH), f32),
            ((TOKENS, WIDTH), f32), ((TOKENS, WIDTH), bf16), ((TOKENS, 128), f32),
            ((TOKENS, WIDTH), f32), ((TOKENS, WIDTH), f32),
            ((TOKENS, HIDDEN), bf16), ((TOKENS, HIDDEN), bf16), ((TOKENS, WIDTH), bf16),
            ((4, 9 * WIDTH, 128), f32),
        ],
        place, pick, spread, cotangent.reshape(TOKENS, WIDTH), *grad_near, tok, mixed,
        out_weight, up_weight, down_weight, vmem=24,
    )
    arrived, returned = to_core(send), give_back(pieces)
    gproj, bias_keep, bias_send = call(
        attend_back_kernel,
        [((TOKENS, 3 * WIDTH), bf16), ((9 * WTOK, 128), bf16), ((9 * WTOK, 128), bf16)],
        [((TOKENS, WIDTH), bf16), ((GTOK, WTOK), f32), ((GTOK, WTOK), bf16), ((2 * HEADS, WTOK, WTOK), f32), ((WTOK, 128), f32)],
        place, proj, probs, gresid, out_weight,
    )
    (gproj, bias_send), (arrived, returned) = after((gproj, bias_send), (arrived, returned))
    bias_arrived = to_core(bias_send)
    others = spread_stage(core_sum(keep, arrived), True)
    qkv_keep, qkv_send = call(
        qkv_grad_kernel,
        [((16 * CHUNK, WIDTH), bf16), ((16 * CHUNK, WIDTH), bf16)],
        [((TOKENS, WIDTH), bf16), ((WIDTH, 3 * WIDTH), f32)],
        place, tok, gproj,
    )
    qkv_arrived = to_core(qkv_send)
    bias_mine = bias_step(low_sum([bias_keep, bias_arrived]), 0)
    gproj, qkv_keep = after((gproj, qkv_keep), ())[0]
    (grad_pieces,) = call(
        token_grad_kernel,
        [((2 * BAND + 2 * SIDE, WIDTH), bf16)],
        [((TOKENS, WIDTH), f32), ((TOKENS, WIDTH), bf16)],
        tok, gproj, qkv_weight, gresid, spread,
    )
    grad_pieces, qkv_arrived, bias_mine, others = after((grad_pieces, qkv_arrived, bias_mine, others), ())[0]
    first = spread_stage(core_sum(qkv_keep, qkv_arrived), True)
    bias_mine = bias_step(bias_mine, 1)
    grad_returned = give_back(grad_pieces)
    first, bias_mine, grad_returned = after((first, bias_mine, grad_returned), ())[0]
    parts = [jnp.concatenate(pair) for pair in zip(cut(low_sum(first), 4), cut(low_sum(others), 4))]
    parts = spread_stage(parts, False)
    bias_mine = bias_step(bias_mine, 2)
    parts, bias_mine = after((parts, bias_mine), ())[0]
    shares = low_sum(parts).reshape(4, CHUNK, WIDTH)
    bias_other = to_core(bias_mine)
    parts = spread_out([lax.dynamic_index_in_dim(shares, (z + by) % 4, 0, False) for by in range(4)], to_z)
    both = jnp.stack([jnp.where(core == 0, bias_mine, bias_other), jnp.where(core == 0, bias_other, bias_mine)])
    wide = both[:, : HEADS * WTOK].reshape(2, HEADS, WTOK, 128)
    tail = both[:, HEADS * WTOK :].reshape(2, WTOK, HEADS, 16).transpose(0, 2, 1, 3)
    bias_grad = jnp.concatenate([wide, tail], axis=3).astype(f32).reshape(1, 2, HEADS, WTOK * WTOK)
    parts, bias_grad = after((parts, bias_grad), ())[0]
    total = total_of(parts)
    by_row = total.reshape(3, 16, WIDTH).transpose(1, 0, 2).reshape(CHUNK, WIDTH)
    total = jnp.where(z == 0, by_row, total)
    weight_grad = total.reshape(-1) * (1.0 / math.sqrt(TOKENS * lax.axis_size("lat") * lax.axis_size("lon")))
    out, grad_latent = assemble(returned), assemble(grad_returned)
    return (out, grad_latent, weight_grad, bias_grad)


def solution(mesh):
    field = P(None, "lat", "lon", None)
    band = P("lat", None, None, None)
    in_specs = (field, field, P(), P(), P(), P(), band)
    out_specs = (field, field, P(("lat", "lon")), band)
    return jax.shard_map(body, mesh=mesh, in_specs=in_specs, out_specs=out_specs, check_vma=False)
```

```python
import functools
import math

import jax
import jax.numpy as jnp
import ml_dtypes
import numpy as np
from jax import lax
from jax.experimental import pallas as pl
from jax.experimental.pallas import tpu as pltpu
from jax.sharding import PartitionSpec as P

WIDTH = 512
HIDDEN = 2048
HEADS = 8
LEVELS = 4
ROWS = 6
COLS = 24
WIN_LEV = 2
WIN_LAT = 6
WIN_LON = 12
WTOK = 144
TOKENS = LEVELS * ROWS * COLS
HALF_LAT = WIN_LAT // 2
HALF_LON = WIN_LON // 2
EDGE = 8
BAND = LEVELS * HALF_LAT * COLS
SIDE = LEVELS * HALF_LAT * EDGE
GROUP = 4
GWIDTH = GROUP * WIDTH // HEADS
GTOK = GROUP * WTOK
WINDOWS = 4
CHUNK = 48
norm_eps = 1e-05
masked_score = -1000000000.0
f32 = jnp.float32
bf16 = jnp.bfloat16


def dot(left, right):
    return lax.dot_general(left, right, (((1,), (0,)), ((), ())), preferred_element_type=f32)


def dot_nt(left, right):
    return lax.dot_general(left, right, (((1,), (1,)), ((), ())), preferred_element_type=f32)


def dot_tn(left, right):
    return lax.dot_general(left, right, (((0,), (0,)), ((), ())), preferred_element_type=f32)


def normalize(values):
    center = values - jnp.mean(values, axis=-1, keepdims=True)
    inv_std = lax.rsqrt(jnp.mean(center * center, axis=-1, keepdims=True) + norm_eps)
    return (center * inv_std, inv_std)


def norm_back(normed, inv_std, upstream):
    mean_grad = jnp.mean(upstream, axis=-1, keepdims=True)
    mean_prod = jnp.mean(upstream * normed, axis=-1, keepdims=True)
    return inv_std * (upstream - mean_grad - normed * mean_prod)


def token_tables():
    pick = np.zeros((TOKENS, TOKENS + BAND + 2 * SIDE), np.float32)
    spread = np.zeros((2 * BAND + 2 * SIDE, TOKENS), np.float32)
    for lev in range(LEVELS):
        src_lev = (lev + 1) % LEVELS
        for i in range(ROWS):
            for j in range(COLS):
                b, lv = divmod(lev, WIN_LEV)
                c, jj = divmod(j, WIN_LON)
                w = (b * 2 + c) * WTOK + (lv * WIN_LAT + i) * WIN_LON + jj
                inner_row = i < HALF_LAT
                inner_col = j < COLS - HALF_LON
                band_row = src_lev * HALF_LAT + (i if inner_row else i - HALF_LAT)
                wide = band_row * COLS + j + HALF_LON
                narrow = band_row * EDGE + j - (COLS - HALF_LON)
                if inner_row and inner_col:
                    pick[w, (src_lev * ROWS + i + HALF_LAT) * COLS + j + HALF_LON] = 1
                    spread[wide, w] = 1
                elif inner_col:
                    pick[w, TOKENS + wide] = 1
                    spread[BAND + wide, w] = 1
                elif inner_row:
                    pick[w, TOKENS + BAND + narrow] = 1
                    spread[2 * BAND + narrow, w] = 1
                else:
                    pick[w, TOKENS + BAND + SIDE + narrow] = 1
                    spread[2 * BAND + SIDE + narrow, w] = 1
    return pick.astype(ml_dtypes.bfloat16), spread.astype(ml_dtypes.bfloat16)


def loop(count, step):
    for i in range(count):
        step(i)


def at(index, size):
    if isinstance(index, int):
        return slice(index * size, (index + 1) * size)
    return pl.ds(pl.multiple_of(index * size, size), size)


def gather_tokens(pick_ref, cat, own_ref, row_ref, col_ref, cor_ref):
    cat[0:TOKENS, :] = own_ref[...]
    cat[TOKENS : TOKENS + BAND, :] = row_ref[...]
    cat[TOKENS + BAND : TOKENS + BAND + SIDE, :] = col_ref[...]
    cat[TOKENS + BAND + SIDE :, :] = cor_ref[...]
    return dot(pick_ref[...], cat[...])


def head_stack(block):
    lane = lax.broadcasted_iota(jnp.int32, block.shape, 1) // (WIDTH // HEADS)
    zero = jnp.zeros_like(block)
    return jnp.concatenate([jnp.where(lane == h, block, zero) for h in range(GROUP)], axis=0)


def head_join(stacked):
    lane = lax.broadcasted_iota(jnp.int32, (WTOK, GWIDTH), 1) // (WIDTH // HEADS)
    total = stacked[0:WTOK]
    for h in range(1, GROUP):
        total = jnp.where(lane == h, stacked[h * WTOK : (h + 1) * WTOK], total)
    return total


def attend_kernel(
    pick_ref, own_ref, row_ref, col_ref, cor_ref, bias_ref, qkv_ref,
    tok_ref, proj_ref, probs_ref, mixed_ref, cat, normed, scores,
):
    scale = (WIDTH // HEADS) ** (-0.5)
    tok_ref[...] = gather_tokens(pick_ref, cat, own_ref, row_ref, col_ref, cor_ref).astype(bf16)

    def norm_rows(i):
        values, _ = normalize(tok_ref[at(i, 48), :].astype(f32))
        normed[at(i, 48), :] = values.astype(bf16)

    loop(TOKENS // 48, norm_rows)

    def project(i):
        proj_ref[:, at(i, 256)] = dot(normed[...], qkv_ref[:, at(i, 256)]).astype(bf16)

    loop(3 * WIDTH // 256, project)

    def attend(i):
        win, group = i // 2, i % 2
        rows = at(win, WTOK)
        query = head_stack(proj_ref[rows, at(group, GWIDTH)])
        scores[...] = dot_nt(query, proj_ref[rows, at(group + 2, GWIDTH)])
        for h in range(GROUP):
            part = scores[h * WTOK : (h + 1) * WTOK, :] * scale + bias_ref[(win // 2) * HEADS + group * GROUP + h]
            expo = jnp.exp(part - jnp.max(part, axis=-1, keepdims=True))
            part = expo * (1.0 / jnp.sum(expo, axis=-1, keepdims=True))
            probs_ref[i, h * WTOK : (h + 1) * WTOK, :] = part.astype(bf16)
        mixed = dot(probs_ref[i], proj_ref[rows, at(group + 4, GWIDTH)])
        mixed_ref[rows, at(group, GWIDTH)] = head_join(mixed).astype(bf16)

    loop(2 * WINDOWS, attend)


def chunk_id(outer, inner, z, place_ref, other):
    core = 1 - place_ref[0] if other else place_ref[0]
    y = lax.rem(place_ref[1] + outer + core * (inner - outer), 4)
    x = lax.rem(place_ref[2] + inner + core * (outer - inner), 4)
    return z * 32 + lax.rem(x, 2) * 16 + (x // 2) * 8 + y * 2 + core


def put_lanes(ref, rows, value):
    for t in range(4):
        ref[t, rows, :] = value[:, t * 128 : (t + 1) * 128]


def mlp_kernel(
    place_ref, pick_ref, spread_ref, own_ref, row_ref, col_ref, cor_ref, tok_ref, mixed_ref,
    out_ref, up_ref, down_ref,
    pieces_ref, gresid_ref, keep_ref, send_ref,
    cat, grad, resid, normed, low, inv, pre, slope, hidden, ghidden, result, wgrad,
):
    grad[...] = gather_tokens(pick_ref, cat, own_ref, row_ref, col_ref, cor_ref).astype(bf16)
    resid[...] = dot(mixed_ref[...], out_ref[...])

    def norm_rows(i):
        rows = at(i, 48)
        total = tok_ref[rows, :].astype(f32) + resid[rows, :]
        resid[rows, :] = total
        values, inv_std = normalize(total)
        normed[rows, :] = values
        inv[rows, :] = jnp.broadcast_to(inv_std, (48, 128))
        low[rows, :] = values.astype(bf16)

    loop(TOKENS // 48, norm_rows)

    def feed(j):
        cols = at(j, WIDTH)
        pre[...] = dot(low[...], up_ref[:, cols])
        slope[...] = dot_nt(grad[...], down_ref[cols, :])

        def gelu(i):
            rows = at(i, 32)
            values = pre[rows, :]
            cumulative = 0.5 * (1.0 + lax.erf(values * 0.7071067811865476))
            hidden[rows, cols] = (values * cumulative).astype(bf16)
            density = jnp.exp(-0.5 * values * values) * 0.3989422804014327
            ghidden[rows, cols] = (slope[rows, :] * (cumulative + values * density)).astype(bf16)

        loop(TOKENS // 32, gelu)
        put_lanes(wgrad, at(j + 5, WIDTH), dot_tn(hidden[:, cols], grad[...]))
        put_lanes(wgrad, pl.ds(WIDTH + j, WIDTH, stride=4), dot_tn(low[...], ghidden[:, cols]))

    for j in range(HIDDEN // WIDTH):
        feed(j)

    def finish(n):
        cols = at(n, 256)
        result[:, cols] = (resid[:, cols] + dot(hidden[...], down_ref[:, cols])).astype(bf16)
        resid[:, cols] = dot_nt(ghidden[...], up_ref[cols, :])

    loop(WIDTH // 256, finish)

    def norm_rows_back(i):
        rows = at(i, 48)
        back = norm_back(normed[rows, :], inv[rows, 0:1], resid[rows, :])
        total = grad[rows, :].astype(f32) + back
        gresid_ref[rows, :] = total
        low[rows, :] = total.astype(bf16)

    loop(TOKENS // 48, norm_rows_back)
    pieces_ref[...] = dot(spread_ref[...], result[...]).astype(bf16)
    put_lanes(wgrad, slice(0, WIDTH), dot_tn(mixed_ref[...], low[...]))

    def share(i):
        for other, ref in ((False, keep_ref), (True, send_ref)):
            chunk = at(chunk_id(i // 12, i // 3 % 4, i % 3, place_ref, other), CHUNK)
            for t in range(4):
                ref[at(i, CHUNK), t * 128 : (t + 1) * 128] = wgrad[t, chunk, :].astype(bf16)

    loop(48, share)


def attend_back_kernel(
    place_ref, proj_ref, probs_ref, gresid_ref, out_ref,
    gproj_ref, keep_ref, send_ref, gmixed, gprobs, gscores, bias, tail,
):
    scale = (WIDTH // HEADS) ** (-0.5)
    gmixed[...] = dot_nt(gresid_ref[...].astype(bf16), out_ref[...]).astype(bf16)

    def back(i):
        lev, group = i // 2, i % 2
        for c in range(2):
            win = lev * 2 + c
            rows = at(win, WTOK)
            probs = win * 2 + group
            upstream = head_stack(gmixed[rows, at(group, GWIDTH)])
            gprobs[...] = dot_nt(upstream, proj_ref[rows, at(group + 4, GWIDTH)])
            for h in range(GROUP):
                part = slice(h * WTOK, (h + 1) * WTOK)
                prob = probs_ref[probs, part, :].astype(f32)
                grads = gprobs[part, :]
                grads = prob * (grads - jnp.sum(grads * prob, axis=-1, keepdims=True))
                gscores[part, :] = (grads * scale).astype(bf16)
                if c == 0:
                    bias[lev * HEADS + group * GROUP + h] = grads
                else:
                    bias[lev * HEADS + group * GROUP + h] += grads
            gproj_ref[rows, at(group + 4, GWIDTH)] = dot_tn(probs_ref[probs], upstream).astype(bf16)
            query = head_stack(proj_ref[rows, at(group, GWIDTH)])
            gproj_ref[rows, at(group + 2, GWIDTH)] = dot_tn(gscores[...], query).astype(bf16)
            gquery = dot(gscores[...], proj_ref[rows, at(group + 2, GWIDTH)])
            gproj_ref[rows, at(group, GWIDTH)] = head_join(gquery).astype(bf16)

    loop(4, back)

    for ref, lev in ((keep_ref, place_ref[0]), (send_ref, 1 - place_ref[0])):
        for h in range(HEADS):
            part = bias[lev * HEADS + h]
            ref[h * WTOK : (h + 1) * WTOK, :] = part[:, :128].astype(bf16)
            tail[:, h * 16 : (h + 1) * 16] = part[:, 128:]
        ref[HEADS * WTOK :, :] = tail[...].astype(bf16)


def qkv_grad_kernel(place_ref, tok_ref, gproj_ref, keep_ref, send_ref, normed, wgrad):
    def norm_rows(i):
        values, _ = normalize(tok_ref[at(i, 48), :].astype(f32))
        normed[at(i, 48), :] = values.astype(bf16)

    loop(TOKENS // 48, norm_rows)

    def product(i):
        wgrad[:, at(i, 512)] = dot_tn(normed[...], gproj_ref[:, at(i, 512)])

    loop(3, product)

    def share(i):
        for other, ref in ((False, keep_ref), (True, send_ref)):
            chunk = at(chunk_id(i // 4, i % 4, 0, place_ref, other), 16)
            for block in range(3):
                ref[at(i * 3 + block, 16), :] = wgrad[chunk, block * WIDTH : (block + 1) * WIDTH].astype(bf16)

    loop(16, share)


def token_grad_kernel(tok_ref, gproj_ref, qkv_ref, gresid_ref, spread_ref, pieces_ref, back, result):
    def product(i):
        back[:, at(i, 256)] = dot_nt(gproj_ref[...], qkv_ref[at(i, 256), :])

    loop(2, product)

    def norm_rows(i):
        rows = at(i, 48)
        values, inv_std = normalize(tok_ref[rows, :].astype(f32))
        result[rows, :] = (gresid_ref[rows, :] + norm_back(values, inv_std, back[rows, :])).astype(bf16)

    loop(TOKENS // 48, norm_rows)
    pieces_ref[...] = dot(spread_ref[...], result[...]).astype(bf16)


def call(kernel, outs, scratch, *operands, vmem=12):
    shapes = [jax.ShapeDtypeStruct(shape, dtype) for shape, dtype in outs]
    specs = [
        pl.BlockSpec(memory_space=pltpu.SMEM if operand.dtype == jnp.int32 else pltpu.VMEM)
        for operand in operands
    ]
    return pl.pallas_call(
        kernel,
        out_shape=shapes,
        in_specs=specs,
        out_specs=[pl.BlockSpec(memory_space=pltpu.VMEM)] * len(outs),
        scratch_shapes=[pltpu.VMEM(shape, dtype) for shape, dtype in scratch],
        compiler_params=pltpu.CompilerParams(vmem_limit_bytes=vmem * 2**20),
        cost_estimate=pl.CostEstimate(flops=2**20, bytes_accessed=2**16, transcendentals=0),
    )(*operands)


def device_index(z, x, y, core):
    return z * 32 + (x % 2) * 16 + (x // 2) * 8 + y * 2 + core


def permute(value, move):
    pairs = []
    for z in range(4):
        for x in range(4):
            for y in range(4):
                for core in range(2):
                    pairs.append((device_index(z, x, y, core), device_index(*move(z, x, y, core))))
    return lax.ppermute(value, ("lat", "lon"), pairs)


def to_core(value):
    return permute(value, lambda z, x, y, core: (z, x, y, 1 - core))


def stage(value, first, by):
    def move(z, x, y, core):
        return (z, x, (y + by) % 4, core) if (core == 0) == first else (z, (x + by) % 4, y, core)

    return permute(value, move)


def to_z(value, by):
    return permute(value, lambda z, x, y, core: ((z + by) % 4, x, y, core))


def bias_step(value, step):
    def move(z, x, y, core):
        kind = (step + 2 * core) % 3
        return ((z, x, y ^ 1, core), (z, x, 3 - y, core), (z, (x + 2) % 4, y, core))[kind]

    return low_sum([value, permute(value, move)])


def shift(value, lat_by, lon_by):
    pairs = []
    for lat in range(8):
        for lon in range(16):
            pairs.append((lat * 16 + lon, (lat + lat_by) % 8 * 16 + (lon + lon_by) % 16))
    return lax.ppermute(value, ("lat", "lon"), pairs)


def total_of(parts):
    total = parts[0].astype(f32)
    for part in parts[1:]:
        total = total + part.astype(f32)
    return total


def cut(value, parts):
    size = value.shape[0] // parts
    return [value[i * size : (i + 1) * size] for i in range(parts)]


def spread_out(parts, move):
    return [parts[0]] + [move(parts[by], by) for by in (1, 2, 3)]


def spread_stage(parts, first):
    return spread_out(parts, lambda value, by: stage(value, first, by))


def core_sum(keep, arrived):
    return [low_sum(pair) for pair in zip(cut(keep, 4), cut(arrived, 4))]


def low_sum(parts):
    return total_of(parts).astype(bf16)


def after(values, others):
    leaves, tree = jax.tree.flatten((values, others))
    return jax.tree.unflatten(tree, lax.optimization_barrier(leaves))


def halos(field):
    band = field[:, :HALF_LAT].reshape(BAND, WIDTH)
    side = field[:, HALF_LAT:, :EDGE].reshape(SIDE, WIDTH)
    corner = field[:, :HALF_LAT, :EDGE].reshape(SIDE, WIDTH)
    return [shift(band, -1, 0), shift(side, 0, -1), shift(corner, -1, -1)]


def give_band(pieces):
    return shift(pieces[BAND : 2 * BAND], 1, 0)


def give_side(pieces):
    return shift(pieces[2 * BAND : 2 * BAND + SIDE], 0, 1)


def give_corner(pieces):
    return shift(pieces[2 * BAND + SIDE :], 1, 1)


def give_back(pieces):
    return [pieces[:BAND], give_band(pieces), give_side(pieces), give_corner(pieces)]


def assemble(parts):
    stay, band = (part.reshape(LEVELS, HALF_LAT, COLS, WIDTH) for part in parts[:2])
    side, corner = (part.reshape(LEVELS, HALF_LAT, EDGE, WIDTH) for part in parts[2:])
    wider = ((0, 0), (0, 0), (0, COLS - EDGE), (0, 0))
    return jnp.concatenate([band + jnp.pad(corner, wider), stay + jnp.pad(side, wider)], axis=1)


def masked_bias(earth_bias):
    token = jnp.arange(WTOK, dtype=jnp.int32)
    wrap_lev = (token >= WTOK // 2).astype(jnp.int32)
    wrap_row = (token % (WTOK // 2) >= HALF_LAT * WIN_LON).astype(jnp.int32)
    wrap_row = wrap_row * (lax.axis_index("lat") == lax.axis_size("lat") - 1).astype(jnp.int32)
    codes = jnp.stack([wrap_row, 2 * wrap_lev + wrap_row])
    allowed = codes[:, :, None] == codes[:, None, :]
    bias = earth_bias.reshape(2, HEADS, WTOK, WTOK)
    return jnp.where(allowed[:, None], bias, masked_score).reshape(2 * HEADS, WTOK, WTOK)


def body(latent, cotangent, qkv_weight, out_weight, up_weight, down_weight, earth_bias):
    lat, lon = lax.axis_index("lat"), lax.axis_index("lon")
    core, y = lon % 2, (lon // 2) % 4
    x, z = (lon // 8) * 2 + lat % 2, lat // 2
    place = jnp.stack([core, y, x]).astype(jnp.int32)
    pick_table, spread_table = token_tables()
    pick, spread = jnp.asarray(pick_table), jnp.asarray(spread_table)

    bias = masked_bias(earth_bias)
    near, grad_near = halos(latent), halos(cotangent)
    tok, proj, probs, mixed = call(
        attend_kernel,
        [((TOKENS, WIDTH), bf16), ((TOKENS, 3 * WIDTH), bf16), ((8, GTOK, WTOK), bf16), ((TOKENS, WIDTH), bf16)],
        [((TOKENS + BAND + 2 * SIDE, WIDTH), bf16), ((TOKENS, WIDTH), bf16), ((GTOK, WTOK), f32)],
        pick, latent.reshape(TOKENS, WIDTH), *near, bias, qkv_weight,
    )
    pieces, gresid, keep, send = call(
        mlp_kernel,
        [
            ((2 * BAND + 2 * SIDE, WIDTH), bf16), ((TOKENS, WIDTH), f32),
            ((48 * CHUNK, WIDTH), bf16), ((48 * CHUNK, WIDTH), bf16),
        ],
        [
            ((TOKENS + BAND + 2 * SIDE, WIDTH), bf16), ((TOKENS, WIDTH), bf16), ((TOKENS, WIDTH), f32),
            ((TOKENS, WIDTH), f32), ((TOKENS, WIDTH), bf16), ((TOKENS, 128), f32),
            ((TOKENS, WIDTH), f32), ((TOKENS, WIDTH), f32),
            ((TOKENS, HIDDEN), bf16), ((TOKENS, HIDDEN), bf16), ((TOKENS, WIDTH), bf16),
            ((4, 9 * WIDTH, 128), f32),
        ],
        place, pick, spread, cotangent.reshape(TOKENS, WIDTH), *grad_near, tok, mixed,
        out_weight, up_weight, down_weight, vmem=24,
    )
    arrived, returned = to_core(send), give_back(pieces)
    gproj, bias_keep, bias_send = call(
        attend_back_kernel,
        [((TOKENS, 3 * WIDTH), bf16), ((9 * WTOK, 128), bf16), ((9 * WTOK, 128), bf16)],
        [((TOKENS, WIDTH), bf16), ((GTOK, WTOK), f32), ((GTOK, WTOK), bf16), ((2 * HEADS, WTOK, WTOK), f32), ((WTOK, 128), f32)],
        place, proj, probs, gresid, out_weight,
    )
    (gproj, bias_send), (arrived, returned) = after((gproj, bias_send), (arrived, returned))
    bias_arrived = to_core(bias_send)
    others = spread_stage(core_sum(keep, arrived), True)
    qkv_keep, qkv_send = call(
        qkv_grad_kernel,
        [((16 * CHUNK, WIDTH), bf16), ((16 * CHUNK, WIDTH), bf16)],
        [((TOKENS, WIDTH), bf16), ((WIDTH, 3 * WIDTH), f32)],
        place, tok, gproj,
    )
    qkv_arrived = to_core(qkv_send)
    bias_mine = bias_step(low_sum([bias_keep, bias_arrived]), 0)
    gproj, qkv_keep = after((gproj, qkv_keep), ())[0]
    (grad_pieces,) = call(
        token_grad_kernel,
        [((2 * BAND + 2 * SIDE, WIDTH), bf16)],
        [((TOKENS, WIDTH), f32), ((TOKENS, WIDTH), bf16)],
        tok, gproj, qkv_weight, gresid, spread,
    )
    grad_pieces, qkv_arrived, bias_mine, others = after((grad_pieces, qkv_arrived, bias_mine, others), ())[0]
    first = spread_stage(core_sum(qkv_keep, qkv_arrived), True)
    bias_mine = bias_step(bias_mine, 1)
    band = give_band(grad_pieces)
    first, bias_mine, band, grad_pieces = after((first, bias_mine, band, grad_pieces), ())[0]
    parts = [jnp.concatenate(pair) for pair in zip(cut(low_sum(first), 4), cut(low_sum(others), 4))]
    parts = spread_stage(parts, False)
    bias_mine = bias_step(bias_mine, 2)
    corner = give_corner(grad_pieces)
    parts, bias_mine, corner, grad_pieces = after((parts, bias_mine, corner, grad_pieces), ())[0]
    side = give_side(grad_pieces)
    shares = low_sum(parts).reshape(4, CHUNK, WIDTH)
    bias_other = to_core(bias_mine)
    parts = spread_out([lax.dynamic_index_in_dim(shares, (z + by) % 4, 0, False) for by in range(4)], to_z)
    both = jnp.stack([jnp.where(core == 0, bias_mine, bias_other), jnp.where(core == 0, bias_other, bias_mine)])
    wide = both[:, : HEADS * WTOK].reshape(2, HEADS, WTOK, 128)
    tail = both[:, HEADS * WTOK :].reshape(2, WTOK, HEADS, 16).transpose(0, 2, 1, 3)
    bias_grad = jnp.concatenate([wide, tail], axis=3).astype(f32).reshape(1, 2, HEADS, WTOK * WTOK)
    parts, bias_grad, side = after((parts, bias_grad, side), ())[0]
    grad_returned = [grad_pieces[:BAND], band, side, corner]
    total = total_of(parts)
    by_row = total.reshape(3, 16, WIDTH).transpose(1, 0, 2).reshape(CHUNK, WIDTH)
    total = jnp.where(z == 0, by_row, total)
    weight_grad = total.reshape(-1) * (1.0 / math.sqrt(TOKENS * lax.axis_size("lat") * lax.axis_size("lon")))
    out, grad_latent = assemble(returned), assemble(grad_returned)
    return (out, grad_latent, weight_grad, bias_grad)


def solution(mesh):
    field = P(None, "lat", "lon", None)
    band = P("lat", None, None, None)
    in_specs = (field, field, P(), P(), P(), P(), band)
    out_specs = (field, field, P(("lat", "lon")), band)
    return jax.shard_map(body, mesh=mesh, in_specs=in_specs, out_specs=out_specs, check_vma=False)
```

```python
import functools
import math

import jax
import jax.numpy as jnp
import ml_dtypes
import numpy as np
from jax import lax
from jax.experimental import pallas as pl
from jax.experimental.pallas import tpu as pltpu
from jax.sharding import PartitionSpec as P

WIDTH = 512
HIDDEN = 2048
HEADS = 8
LEVELS = 4
ROWS = 6
COLS = 24
WIN_LEV = 2
WIN_LAT = 6
WIN_LON = 12
WTOK = 144
TOKENS = LEVELS * ROWS * COLS
HALF_LAT = WIN_LAT // 2
HALF_LON = WIN_LON // 2
EDGE = 8
BAND = LEVELS * HALF_LAT * COLS
SIDE = LEVELS * HALF_LAT * EDGE
GROUP = 4
GWIDTH = GROUP * WIDTH // HEADS
GTOK = GROUP * WTOK
WINDOWS = 4
CHUNK = 48
norm_eps = 1e-05
masked_score = -1000000000.0
f32 = jnp.float32
bf16 = jnp.bfloat16


def dot(left, right):
    return lax.dot_general(left, right, (((1,), (0,)), ((), ())), preferred_element_type=f32)


def dot_nt(left, right):
    return lax.dot_general(left, right, (((1,), (1,)), ((), ())), preferred_element_type=f32)


def dot_tn(left, right):
    return lax.dot_general(left, right, (((0,), (0,)), ((), ())), preferred_element_type=f32)


def normalize(values):
    center = values - jnp.mean(values, axis=-1, keepdims=True)
    inv_std = lax.rsqrt(jnp.mean(center * center, axis=-1, keepdims=True) + norm_eps)
    return (center * inv_std, inv_std)


def norm_back(normed, inv_std, upstream):
    mean_grad = jnp.mean(upstream, axis=-1, keepdims=True)
    mean_prod = jnp.mean(upstream * normed, axis=-1, keepdims=True)
    return inv_std * (upstream - mean_grad - normed * mean_prod)


def token_tables():
    pick = np.zeros((TOKENS, TOKENS + BAND + 2 * SIDE), np.float32)
    spread = np.zeros((2 * BAND + 2 * SIDE, TOKENS), np.float32)
    for lev in range(LEVELS):
        src_lev = (lev + 1) % LEVELS
        for i in range(ROWS):
            for j in range(COLS):
                b, lv = divmod(lev, WIN_LEV)
                c, jj = divmod(j, WIN_LON)
                w = (b * 2 + c) * WTOK + (lv * WIN_LAT + i) * WIN_LON + jj
                inner_row = i < HALF_LAT
                inner_col = j < COLS - HALF_LON
                band_row = src_lev * HALF_LAT + (i if inner_row else i - HALF_LAT)
                wide = band_row * COLS + j + HALF_LON
                narrow = band_row * EDGE + j - (COLS - HALF_LON)
                if inner_row and inner_col:
                    pick[w, (src_lev * ROWS + i + HALF_LAT) * COLS + j + HALF_LON] = 1
                    spread[wide, w] = 1
                elif inner_col:
                    pick[w, TOKENS + wide] = 1
                    spread[BAND + wide, w] = 1
                elif inner_row:
                    pick[w, TOKENS + BAND + narrow] = 1
                    spread[2 * BAND + SIDE + narrow, w] = 1
                else:
                    pick[w, TOKENS + BAND + SIDE + narrow] = 1
                    spread[2 * BAND + narrow, w] = 1
    return pick.astype(ml_dtypes.bfloat16), spread.astype(ml_dtypes.bfloat16)


def loop(count, step):
    for i in range(count):
        step(i)


def at(index, size):
    if isinstance(index, int):
        return slice(index * size, (index + 1) * size)
    return pl.ds(pl.multiple_of(index * size, size), size)


def gather_tokens(pick_ref, cat, own_ref, row_ref, col_ref, cor_ref):
    cat[0:TOKENS, :] = own_ref[...]
    cat[TOKENS : TOKENS + BAND, :] = row_ref[...]
    cat[TOKENS + BAND : TOKENS + BAND + SIDE, :] = col_ref[...]
    cat[TOKENS + BAND + SIDE :, :] = cor_ref[...]
    return dot(pick_ref[...], cat[...])


def head_stack(block):
    lane = lax.broadcasted_iota(jnp.int32, block.shape, 1) // (WIDTH // HEADS)
    zero = jnp.zeros_like(block)
    return jnp.concatenate([jnp.where(lane == h, block, zero) for h in range(GROUP)], axis=0)


def head_join(stacked):
    lane = lax.broadcasted_iota(jnp.int32, (WTOK, GWIDTH), 1) // (WIDTH // HEADS)
    total = stacked[0:WTOK]
    for h in range(1, GROUP):
        total = jnp.where(lane == h, stacked[h * WTOK : (h + 1) * WTOK], total)
    return total


def attend_kernel(
    pick_ref, own_ref, row_ref, col_ref, cor_ref, bias_ref, qkv_ref,
    tok_ref, proj_ref, probs_ref, mixed_ref, cat, normed, scores,
):
    scale = (WIDTH // HEADS) ** (-0.5)
    tok_ref[...] = gather_tokens(pick_ref, cat, own_ref, row_ref, col_ref, cor_ref).astype(bf16)

    def norm_rows(i):
        values, _ = normalize(tok_ref[at(i, 48), :].astype(f32))
        normed[at(i, 48), :] = values.astype(bf16)

    loop(TOKENS // 48, norm_rows)

    def project(i):
        proj_ref[:, at(i, 256)] = dot(normed[...], qkv_ref[:, at(i, 256)]).astype(bf16)

    loop(3 * WIDTH // 256, project)

    def attend(i):
        win, group = i // 2, i % 2
        rows = at(win, WTOK)
        query = head_stack(proj_ref[rows, at(group, GWIDTH)])
        scores[...] = dot_nt(query, proj_ref[rows, at(group + 2, GWIDTH)])
        for h in range(GROUP):
            part = scores[h * WTOK : (h + 1) * WTOK, :] * scale + bias_ref[(win // 2) * HEADS + group * GROUP + h]
            expo = jnp.exp(part - jnp.max(part, axis=-1, keepdims=True))
            part = expo * (1.0 / jnp.sum(expo, axis=-1, keepdims=True))
            probs_ref[i, h * WTOK : (h + 1) * WTOK, :] = part.astype(bf16)
        mixed = dot(probs_ref[i], proj_ref[rows, at(group + 4, GWIDTH)])
        mixed_ref[rows, at(group, GWIDTH)] = head_join(mixed).astype(bf16)

    loop(2 * WINDOWS, attend)


def chunk_id(outer, inner, z, place_ref, other):
    core = 1 - place_ref[0] if other else place_ref[0]
    y = lax.rem(place_ref[1] + outer + core * (inner - outer), 4)
    x = lax.rem(place_ref[2] + inner + core * (outer - inner), 4)
    return z * 32 + lax.rem(x, 2) * 16 + (x // 2) * 8 + y * 2 + core


def put_lanes(ref, rows, value):
    for t in range(4):
        ref[t, rows, :] = value[:, t * 128 : (t + 1) * 128]


def mlp_kernel(
    place_ref, pick_ref, spread_ref, own_ref, row_ref, col_ref, cor_ref, tok_ref, mixed_ref,
    out_ref, up_ref, down_ref,
    pieces_ref, gresid_ref, keep_ref, send_ref,
    cat, grad, resid, normed, low, inv, pre, slope, hidden, ghidden, result, wgrad,
):
    grad[...] = gather_tokens(pick_ref, cat, own_ref, row_ref, col_ref, cor_ref).astype(bf16)
    resid[...] = dot(mixed_ref[...], out_ref[...])

    def norm_rows(i):
        rows = at(i, 48)
        total = tok_ref[rows, :].astype(f32) + resid[rows, :]
        resid[rows, :] = total
        values, inv_std = normalize(total)
        normed[rows, :] = values
        inv[rows, :] = jnp.broadcast_to(inv_std, (48, 128))
        low[rows, :] = values.astype(bf16)

    loop(TOKENS // 48, norm_rows)

    def feed(j):
        cols = at(j, WIDTH)
        pre[...] = dot(low[...], up_ref[:, cols])
        slope[...] = dot_nt(grad[...], down_ref[cols, :])

        def gelu(i):
            rows = at(i, 32)
            values = pre[rows, :]
            cumulative = 0.5 * (1.0 + lax.erf(values * 0.7071067811865476))
            hidden[rows, cols] = (values * cumulative).astype(bf16)
            density = jnp.exp(-0.5 * values * values) * 0.3989422804014327
            ghidden[rows, cols] = (slope[rows, :] * (cumulative + values * density)).astype(bf16)

        loop(TOKENS // 32, gelu)
        put_lanes(wgrad, at(j + 5, WIDTH), dot_tn(hidden[:, cols], grad[...]))
        put_lanes(wgrad, pl.ds(WIDTH + j, WIDTH, stride=4), dot_tn(low[...], ghidden[:, cols]))

    for j in range(HIDDEN // WIDTH):
        feed(j)

    def finish(n):
        cols = at(n, 256)
        result[:, cols] = (resid[:, cols] + dot(hidden[...], down_ref[:, cols])).astype(bf16)
        resid[:, cols] = dot_nt(ghidden[...], up_ref[cols, :])

    loop(WIDTH // 256, finish)

    def norm_rows_back(i):
        rows = at(i, 48)
        back = norm_back(normed[rows, :], inv[rows, 0:1], resid[rows, :])
        total = grad[rows, :].astype(f32) + back
        gresid_ref[rows, :] = total
        low[rows, :] = total.astype(bf16)

    loop(TOKENS // 48, norm_rows_back)
    pieces_ref[...] = dot(spread_ref[...], result[...]).astype(bf16)
    put_lanes(wgrad, slice(0, WIDTH), dot_tn(mixed_ref[...], low[...]))

    def share(i):
        for other, ref in ((False, keep_ref), (True, send_ref)):
            chunk = at(chunk_id(i // 12, i // 3 % 4, i % 3, place_ref, other), CHUNK)
            for t in range(4):
                ref[at(i, CHUNK), t * 128 : (t + 1) * 128] = wgrad[t, chunk, :].astype(bf16)

    loop(48, share)


def attend_back_kernel(
    place_ref, proj_ref, probs_ref, gresid_ref, out_ref,
    gproj_ref, keep_ref, send_ref, gmixed, gprobs, gscores, bias, tail,
):
    scale = (WIDTH // HEADS) ** (-0.5)
    gmixed[...] = dot_nt(gresid_ref[...].astype(bf16), out_ref[...]).astype(bf16)

    def back(i):
        lev, group = i // 2, i % 2
        for c in range(2):
            win = lev * 2 + c
            rows = at(win, WTOK)
            probs = win * 2 + group
            upstream = head_stack(gmixed[rows, at(group, GWIDTH)])
            gprobs[...] = dot_nt(upstream, proj_ref[rows, at(group + 4, GWIDTH)])
            for h in range(GROUP):
                part = slice(h * WTOK, (h + 1) * WTOK)
                prob = probs_ref[probs, part, :].astype(f32)
                grads = gprobs[part, :]
                grads = prob * (grads - jnp.sum(grads * prob, axis=-1, keepdims=True))
                gscores[part, :] = (grads * scale).astype(bf16)
                if c == 0:
                    bias[lev * HEADS + group * GROUP + h] = grads
                else:
                    bias[lev * HEADS + group * GROUP + h] += grads
            gproj_ref[rows, at(group + 4, GWIDTH)] = dot_tn(probs_ref[probs], upstream).astype(bf16)
            query = head_stack(proj_ref[rows, at(group, GWIDTH)])
            gproj_ref[rows, at(group + 2, GWIDTH)] = dot_tn(gscores[...], query).astype(bf16)
            gquery = dot(gscores[...], proj_ref[rows, at(group + 2, GWIDTH)])
            gproj_ref[rows, at(group, GWIDTH)] = head_join(gquery).astype(bf16)

    loop(4, back)

    for ref, lev in ((keep_ref, place_ref[0]), (send_ref, 1 - place_ref[0])):
        for h in range(HEADS):
            part = bias[lev * HEADS + h]
            ref[h * WTOK : (h + 1) * WTOK, :] = part[:, :128].astype(bf16)
            tail[:, h * 16 : (h + 1) * 16] = part[:, 128:]
        ref[HEADS * WTOK :, :] = tail[...].astype(bf16)


def qkv_grad_kernel(place_ref, tok_ref, gproj_ref, keep_ref, send_ref, normed, wgrad):
    def norm_rows(i):
        values, _ = normalize(tok_ref[at(i, 48), :].astype(f32))
        normed[at(i, 48), :] = values.astype(bf16)

    loop(TOKENS // 48, norm_rows)

    def product(i):
        wgrad[:, at(i, 512)] = dot_tn(normed[...], gproj_ref[:, at(i, 512)])

    loop(3, product)

    def share(i):
        for other, ref in ((False, keep_ref), (True, send_ref)):
            chunk = at(chunk_id(i // 4, i % 4, 0, place_ref, other), 16)
            for block in range(3):
                ref[at(i * 3 + block, 16), :] = wgrad[chunk, block * WIDTH : (block + 1) * WIDTH].astype(bf16)

    loop(16, share)


def token_grad_kernel(tok_ref, gproj_ref, qkv_ref, gresid_ref, spread_ref, pieces_ref, back, result):
    def product(i):
        back[:, at(i, 256)] = dot_nt(gproj_ref[...], qkv_ref[at(i, 256), :])

    loop(2, product)

    def norm_rows(i):
        rows = at(i, 48)
        values, inv_std = normalize(tok_ref[rows, :].astype(f32))
        result[rows, :] = (gresid_ref[rows, :] + norm_back(values, inv_std, back[rows, :])).astype(bf16)

    loop(TOKENS // 48, norm_rows)
    pieces_ref[...] = dot(spread_ref[...], result[...]).astype(bf16)


def call(kernel, outs, scratch, *operands, vmem=12):
    shapes = [jax.ShapeDtypeStruct(shape, dtype) for shape, dtype in outs]
    specs = [
        pl.BlockSpec(memory_space=pltpu.SMEM if operand.dtype == jnp.int32 else pltpu.VMEM)
        for operand in operands
    ]
    return pl.pallas_call(
        kernel,
        out_shape=shapes,
        in_specs=specs,
        out_specs=[pl.BlockSpec(memory_space=pltpu.VMEM)] * len(outs),
        scratch_shapes=[pltpu.VMEM(shape, dtype) for shape, dtype in scratch],
        compiler_params=pltpu.CompilerParams(vmem_limit_bytes=vmem * 2**20),
        cost_estimate=pl.CostEstimate(flops=2**20, bytes_accessed=2**16, transcendentals=0),
    )(*operands)


def device_index(z, x, y, core):
    return z * 32 + (x % 2) * 16 + (x // 2) * 8 + y * 2 + core


def permute(value, move):
    pairs = []
    for z in range(4):
        for x in range(4):
            for y in range(4):
                for core in range(2):
                    pairs.append((device_index(z, x, y, core), device_index(*move(z, x, y, core))))
    return lax.ppermute(value, ("lat", "lon"), pairs)


def to_core(value):
    return permute(value, lambda z, x, y, core: (z, x, y, 1 - core))


def stage(value, first, by):
    def move(z, x, y, core):
        return (z, x, (y + by) % 4, core) if (core == 0) == first else (z, (x + by) % 4, y, core)

    return permute(value, move)


def to_z(value, by):
    return permute(value, lambda z, x, y, core: ((z + by) % 4, x, y, core))


def bias_step(value, step):
    def move(z, x, y, core):
        kind = (step + 2 * core) % 3
        return ((z, x, y ^ 1, core), (z, x, 3 - y, core), (z, (x + 2) % 4, y, core))[kind]

    return low_sum([value, permute(value, move)])


def shift(value, lat_by, lon_by):
    pairs = []
    for lat in range(8):
        for lon in range(16):
            pairs.append((lat * 16 + lon, (lat + lat_by) % 8 * 16 + (lon + lon_by) % 16))
    return lax.ppermute(value, ("lat", "lon"), pairs)


def total_of(parts):
    total = parts[0].astype(f32)
    for part in parts[1:]:
        total = total + part.astype(f32)
    return total


def cut(value, parts):
    size = value.shape[0] // parts
    return [value[i * size : (i + 1) * size] for i in range(parts)]


def spread_out(parts, move):
    return [parts[0]] + [move(parts[by], by) for by in (1, 2, 3)]


def spread_stage(parts, first):
    return spread_out(parts, lambda value, by: stage(value, first, by))


def core_sum(keep, arrived):
    return [low_sum(pair) for pair in zip(cut(keep, 4), cut(arrived, 4))]


def low_sum(parts):
    return total_of(parts).astype(bf16)


def after(values, others):
    leaves, tree = jax.tree.flatten((values, others))
    return jax.tree.unflatten(tree, lax.optimization_barrier(leaves))


def halos(field):
    band = field[:, :HALF_LAT].reshape(BAND, WIDTH)
    side = field[:, HALF_LAT:, :EDGE].reshape(SIDE, WIDTH)
    corner = field[:, :HALF_LAT, :EDGE].reshape(SIDE, WIDTH)
    return [shift(band, -1, 0), shift(side, 0, -1), shift(corner, -1, -1)]


def give_band(pieces):
    return shift(pieces[BAND : 2 * BAND], 1, 0)


def give_back(pieces):
    side = shift(pieces[2 * BAND + SIDE :], 0, 1)
    return [pieces[:BAND], give_band(pieces), side, shift(pieces[2 * BAND : 2 * BAND + SIDE], 1, 1)]


def assemble(parts):
    stay, band = (part.reshape(LEVELS, HALF_LAT, COLS, WIDTH) for part in parts[:2])
    side, corner = (part.reshape(LEVELS, HALF_LAT, EDGE, WIDTH) for part in parts[2:])
    wider = ((0, 0), (0, 0), (0, COLS - EDGE), (0, 0))
    return jnp.concatenate([band + jnp.pad(corner, wider), stay + jnp.pad(side, wider)], axis=1)


def masked_bias(earth_bias):
    token = jnp.arange(WTOK, dtype=jnp.int32)
    wrap_lev = (token >= WTOK // 2).astype(jnp.int32)
    wrap_row = (token % (WTOK // 2) >= HALF_LAT * WIN_LON).astype(jnp.int32)
    wrap_row = wrap_row * (lax.axis_index("lat") == lax.axis_size("lat") - 1).astype(jnp.int32)
    codes = jnp.stack([wrap_row, 2 * wrap_lev + wrap_row])
    allowed = codes[:, :, None] == codes[:, None, :]
    bias = earth_bias.reshape(2, HEADS, WTOK, WTOK)
    return jnp.where(allowed[:, None], bias, masked_score).reshape(2 * HEADS, WTOK, WTOK)


def body(latent, cotangent, qkv_weight, out_weight, up_weight, down_weight, earth_bias):
    lat, lon = lax.axis_index("lat"), lax.axis_index("lon")
    core, y = lon % 2, (lon // 2) % 4
    x, z = (lon // 8) * 2 + lat % 2, lat // 2
    place = jnp.stack([core, y, x]).astype(jnp.int32)
    pick_table, spread_table = token_tables()
    pick, spread = jnp.asarray(pick_table), jnp.asarray(spread_table)

    bias = masked_bias(earth_bias)
    near, grad_near = halos(latent), halos(cotangent)
    tok, proj, probs, mixed = call(
        attend_kernel,
        [((TOKENS, WIDTH), bf16), ((TOKENS, 3 * WIDTH), bf16), ((8, GTOK, WTOK), bf16), ((TOKENS, WIDTH), bf16)],
        [((TOKENS + BAND + 2 * SIDE, WIDTH), bf16), ((TOKENS, WIDTH), bf16), ((GTOK, WTOK), f32)],
        pick, latent.reshape(TOKENS, WIDTH), *near, bias, qkv_weight,
    )
    pieces, gresid, keep, send = call(
        mlp_kernel,
        [
            ((2 * BAND + 2 * SIDE, WIDTH), bf16), ((TOKENS, WIDTH), f32),
            ((48 * CHUNK, WIDTH), bf16), ((48 * CHUNK, WIDTH), bf16),
        ],
        [
            ((TOKENS + BAND + 2 * SIDE, WIDTH), bf16), ((TOKENS, WIDTH), bf16), ((TOKENS, WIDTH), f32),
            ((TOKENS, WIDTH), f32), ((TOKENS, WIDTH), bf16), ((TOKENS, 128), f32),
            ((TOKENS, WIDTH), f32), ((TOKENS, WIDTH), f32),
            ((TOKENS, HIDDEN), bf16), ((TOKENS, HIDDEN), bf16), ((TOKENS, WIDTH), bf16),
            ((4, 9 * WIDTH, 128), f32),
        ],
        place, pick, spread, cotangent.reshape(TOKENS, WIDTH), *grad_near, tok, mixed,
        out_weight, up_weight, down_weight, vmem=24,
    )
    arrived, returned = to_core(send), give_back(pieces)
    gproj, bias_keep, bias_send = call(
        attend_back_kernel,
        [((TOKENS, 3 * WIDTH), bf16), ((9 * WTOK, 128), bf16), ((9 * WTOK, 128), bf16)],
        [((TOKENS, WIDTH), bf16), ((GTOK, WTOK), f32), ((GTOK, WTOK), bf16), ((2 * HEADS, WTOK, WTOK), f32), ((WTOK, 128), f32)],
        place, proj, probs, gresid, out_weight,
    )
    (gproj, bias_send), (arrived, returned) = after((gproj, bias_send), (arrived, returned))
    bias_arrived = to_core(bias_send)
    others = spread_stage(core_sum(keep, arrived), True)
    qkv_keep, qkv_send = call(
        qkv_grad_kernel,
        [((16 * CHUNK, WIDTH), bf16), ((16 * CHUNK, WIDTH), bf16)],
        [((TOKENS, WIDTH), bf16), ((WIDTH, 3 * WIDTH), f32)],
        place, tok, gproj,
    )
    qkv_arrived = to_core(qkv_send)
    bias_mine = bias_step(low_sum([bias_keep, bias_arrived]), 0)
    gproj, qkv_keep = after((gproj, qkv_keep), ())[0]
    (grad_pieces,) = call(
        token_grad_kernel,
        [((2 * BAND + 2 * SIDE, WIDTH), bf16)],
        [((TOKENS, WIDTH), f32), ((TOKENS, WIDTH), bf16)],
        tok, gproj, qkv_weight, gresid, spread,
    )
    grad_pieces, qkv_arrived, bias_mine, others = after((grad_pieces, qkv_arrived, bias_mine, others), ())[0]
    first = spread_stage(core_sum(qkv_keep, qkv_arrived), True)
    bias_mine = bias_step(bias_mine, 1)
    band = shift(grad_pieces[BAND : 2 * BAND + SIDE], 1, 0)
    first, bias_mine, band, grad_pieces = after((first, bias_mine, band, grad_pieces), ())[0]
    parts = [jnp.concatenate(pair) for pair in zip(cut(low_sum(first), 4), cut(low_sum(others), 4))]
    parts = spread_stage(parts, False)
    bias_mine = bias_step(bias_mine, 2)
    edges = jnp.concatenate([grad_pieces[2 * BAND + SIDE :], band[BAND:]])
    parts, bias_mine, edges = after((parts, bias_mine, edges), ())[0]
    edges = shift(edges, 0, 1)
    shares = low_sum(parts).reshape(4, CHUNK, WIDTH)
    bias_other = to_core(bias_mine)
    parts = spread_out([lax.dynamic_index_in_dim(shares, (z + by) % 4, 0, False) for by in range(4)], to_z)
    both = jnp.stack([jnp.where(core == 0, bias_mine, bias_other), jnp.where(core == 0, bias_other, bias_mine)])
    wide = both[:, : HEADS * WTOK].reshape(2, HEADS, WTOK, 128)
    tail = both[:, HEADS * WTOK :].reshape(2, WTOK, HEADS, 16).transpose(0, 2, 1, 3)
    bias_grad = jnp.concatenate([wide, tail], axis=3).astype(f32).reshape(1, 2, HEADS, WTOK * WTOK)
    parts, bias_grad, edges = after((parts, bias_grad, edges), ())[0]
    grad_returned = [grad_pieces[:BAND], band[:BAND], edges[:SIDE], edges[SIDE:]]
    total = total_of(parts)
    by_row = total.reshape(3, 16, WIDTH).transpose(1, 0, 2).reshape(CHUNK, WIDTH)
    total = jnp.where(z == 0, by_row, total)
    weight_grad = total.reshape(-1) * (1.0 / math.sqrt(TOKENS * lax.axis_size("lat") * lax.axis_size("lon")))
    out, grad_latent = assemble(returned), assemble(grad_returned)
    return (out, grad_latent, weight_grad, bias_grad)


def solution(mesh):
    field = P(None, "lat", "lon", None)
    band = P("lat", None, None, None)
    in_specs = (field, field, P(), P(), P(), P(), band)
    out_specs = (field, field, P(("lat", "lon")), band)
    return jax.shard_map(body, mesh=mesh, in_specs=in_specs, out_specs=out_specs, check_vma=False)
```
